128 devices in a mesh: group: 2 (over y_lo), lat: 8 (over y_hi, z), lon: 8 (over x, core).
Axes of the slice: x: 4, y: 4 (y_hi: 2, y_lo: 2; y = y_hi * 2 + y_lo), z: 4, core: 2. Of those that a mesh axis runs over, the one named last changes fastest.
Arguments:
- atmos: bfloat16 [256, 720, 1024], P('group', 'lat', 'lon'), may hold values from -6 to 6
- cotangent: bfloat16 [256, 720, 1024], P('group', 'lat', 'lon'), may hold values from -6 to 6
- ocean: bfloat16 [76, 720, 1024], P(None, 'lat', 'lon'), may hold values from -6 to 6
- sea_mask: int32 [720, 1024], P('lat', 'lon'), may hold values 0 or 1
- spectral_weight: float32 [256, 384], P(('group', 'lat', 'lon')), may hold values from -5 to 5
- coupling: float32 [256], P('group'), may hold values from -5 to 5
- flux_weight: bfloat16 [4, 256], P(None, 'group'), may hold values from -0.375 to 0.375
- conv_weight: bfloat16 [3, 3, 80, 256], P(None, None, None, 'group'), may hold values from -0.21875 to 0.21875
- head_weight: bfloat16 [256, 76], P('group'), may hold values from -0.375 to 0.375
Outputs:
- atmos_next: bfloat16 [256, 720, 1024], P('group', 'lat', 'lon')
- grad_atmos: bfloat16 [256, 720, 1024], P('group', 'lat', 'lon')
- grad_spectral: float32 [256, 384], P(('group', 'lat', 'lon'))
- ocean_next: bfloat16 [76, 720, 1024], P(None, 'lat', 'lon')
The draws below stay inside these ranges and needn't reach their ends.
All inputs are finite; a program needn't handle non-finite values. No bound on the sum of `sea_mask` on one device may be relied on, other than what follows from the above.
Results may differ from the reference program's by a relative error of at most 0.012.
Values may be sent and summed in bfloat16 or wider, within the bound.
No kernel may reach another device: no remote copies, remote signals or barrier semaphores. Data moves between devices by JAX's collectives and lax.ppermute only.
A program may use at most 192 MiB of HBM per device.

```python
import math
import jax
import jax.numpy as jnp
from jax import lax

C = 256
NLAT = 720
NLON = 1024
KMODES = 384
LDEG = 384
OC = 76
NF = 4
HID = 256
OIN = 80


def place_ends(drawn, key, smallest, top_value):
    index_at = [jax.random.randint(jax.random.fold_in(key, axis), (), 0, length) for axis, length in enumerate(drawn.shape)]
    widest = drawn.shape.index(max(drawn.shape))
    neighbour = index_at[:widest] + [(index_at[widest] + 1) % drawn.shape[widest]] + index_at[widest + 1:]
    return drawn.at[tuple(index_at)].set(smallest).at[tuple(neighbour)].set(top_value)


def block_scale(own_key, extent, cuts, low, high):
    factor_of = 1.0
    for dim, parts in cuts:
        heights = jax.random.uniform(jax.random.fold_in(jax.random.fold_in(own_key, 6), dim), (parts,), jnp.float32, low / len(cuts), high / len(cuts))
        factor_of = factor_of * jnp.repeat(jnp.exp(heights), extent[dim] // parts).reshape((-1,) + (1,) * (len(extent) - 1 - dim))
    return factor_of


def centred(stream_key, dims, scale, reach, pieces=(), kind=jnp.bfloat16):
    drawn = jax.random.normal(stream_key, dims, jnp.float32) * scale
    if len(pieces) > 0:
        drawn = block_scale(stream_key, dims, pieces, -0.22, 0.18) * drawn
    return jnp.clip(drawn, min=-reach, max=reach).astype(kind)


def setup_inputs(seed: int = 0) -> dict:
    splits = jax.random.split(jax.random.key(seed), 10)
    atmos = centred(splits[0], (C, NLAT, NLON), 1.0, 6.0, ((0, 2), (1, 8), (2, 8)))
    cotangent = centred(splits[1], (C, NLAT, NLON), 1.0, 6.0, ((0, 2), (1, 8), (2, 8)))
    ocean = centred(splits[2], (OC, NLAT, NLON), 1.0, 6.0, ((1, 8), (2, 8)))
    sea_mask = place_ends((jax.random.randint(splits[3], (NLAT, NLON), 0, 10) < 7).astype(jnp.int32), jax.random.fold_in(splits[3], 1), 0, 1)
    spectral_weight = centred(splits[4], (C, LDEG), 1.0, 5.0, ((0, 128),), jnp.float32)
    coupling = centred(splits[5], (C,), 1.0, 5.0, ((0, 2),), jnp.float32)
    flux_weight = centred(splits[6], (NF, C), C ** -0.5, 0.375, ((1, 2),))
    conv_weight = centred(splits[7], (3, 3, OIN, HID), (9 * OIN) ** -0.5, 0.21875, ((3, 2),))
    head_weight = centred(splits[8], (HID, OC), HID ** -0.5, 0.375, ((0, 2),))
    return dict(atmos=atmos, cotangent=cotangent, ocean=ocean, sea_mask=sea_mask, spectral_weight=spectral_weight, coupling=coupling, flux_weight=flux_weight, conv_weight=conv_weight, head_weight=head_weight)


def make_tables(nlat, nlon, kmodes, ldeg):
    column = jnp.arange(nlon, dtype=jnp.int32)[:, None]
    wavenum = jnp.arange(kmodes, dtype=jnp.int32)[None, :]
    phase_cos = (column * wavenum % nlon).astype(jnp.float32) * (2.0 * math.pi / nlon)
    phase_sin = (column * (wavenum + 1) % nlon).astype(jnp.float32) * (2.0 * math.pi / nlon)
    lon_table = (jnp.concatenate([jnp.cos(phase_cos), jnp.sin(phase_sin)], axis=1) * math.sqrt(2.0 / nlon)).astype(jnp.bfloat16)
    latrow = jnp.arange(nlat, dtype=jnp.int32)[:, None]
    degree = jnp.arange(ldeg, dtype=jnp.int32)[None, :]
    phase_lat = (degree * (2 * latrow + 1) % (4 * nlat)).astype(jnp.float32) * (math.pi / (2 * nlat))
    lat_table = (jnp.cos(phase_lat) * math.sqrt(2.0 / nlat)).astype(jnp.bfloat16)
    return (lon_table, lat_table)

def reference(atmos, cotangent, ocean, sea_mask, spectral_weight, coupling, flux_weight, conv_weight, head_weight):
    sea_cells = sea_mask.astype(jnp.float32)
    atmos_input = (atmos.astype(jnp.float32) + sea_cells[None] * ocean[0].astype(jnp.float32)[None] * coupling[:, None, None]).astype(jnp.bfloat16)
    fields = jnp.stack([atmos_input, cotangent])
    lon_table, lat_table = make_tables(NLAT, NLON, KMODES, LDEG)
    lon_wide = lon_table.astype(jnp.float32)
    lat_wide = lat_table.astype(jnp.float32)
    cblock = math.gcd(C, 16)
    nblock = C // cblock
    grouped = fields.reshape(2, nblock, cblock, NLAT, NLON).transpose(1, 0, 2, 3, 4)
    weight_groups = spectral_weight.reshape(nblock, cblock, LDEG)

    def one_block(pair):
        block_fields, block_weight = pair
        lon_coef = lax.optimization_barrier(jnp.einsum('fcan,nk->fcak', block_fields.astype(jnp.float32), lon_wide).astype(jnp.bfloat16))
        spectra = jnp.einsum('fcak,al->fclk', lon_coef.astype(jnp.float32), lat_wide)
        filtered = lax.optimization_barrier((spectra * block_weight[None, :, :, None]).astype(jnp.bfloat16))
        lat_back = lax.optimization_barrier(jnp.einsum('fclk,al->fcak', filtered.astype(jnp.float32), lat_wide).astype(jnp.bfloat16))
        back = jnp.einsum('fcak,nk->fcan', lat_back.astype(jnp.float32), lon_wide).astype(jnp.bfloat16)
        grad = lax.optimization_barrier(jnp.sum(spectra[0] * spectra[1], axis=-1)) / KMODES
        return (back, grad)
    backs, grads = lax.map(one_block, (grouped, weight_groups))
    back = backs.transpose(1, 0, 2, 3, 4).reshape(2, C, NLAT, NLON)
    grad_spectral = grads.reshape(C, LDEG)
    atmos_next = (atmos_input.astype(jnp.float32) + back[0].astype(jnp.float32)).astype(jnp.bfloat16)
    grad_atmos = (cotangent.astype(jnp.float32) + back[1].astype(jnp.float32)).astype(jnp.bfloat16)
    flux = jnp.dot(flux_weight, atmos_next.reshape(C, NLAT * NLON), preferred_element_type=jnp.float32)
    flux = flux.reshape(NF, NLAT, NLON).astype(jnp.bfloat16)
    ocean_input = jnp.concatenate([ocean, flux], axis=0)
    padded = jnp.pad(ocean_input, ((0, 0), (1, 1), (0, 0)))
    padded = jnp.concatenate([padded[:, :, -1:], padded, padded[:, :, :1]], axis=2)
    padded_wide = padded.astype(jnp.float32)
    hblock = math.gcd(HID, 32)
    hcount = HID // hblock
    conv_groups = conv_weight.reshape(3, 3, OIN, hcount, hblock).transpose(3, 0, 1, 2, 4)
    head_groups = head_weight.reshape(hcount, hblock, OC)

    def add_block(total, pair):
        conv_part, head_part = pair
        summed = jnp.zeros((hblock, NLAT, NLON), jnp.float32)
        for row_shift in range(3):
            for col_shift in range(3):
                window = padded_wide[:, row_shift:row_shift + NLAT, col_shift:col_shift + NLON]
                summed = summed + jnp.einsum('irq,ih->hrq', window, conv_part[row_shift, col_shift].astype(jnp.float32))
        hidden = lax.optimization_barrier(jax.nn.gelu(summed).astype(jnp.bfloat16))
        return (total + jnp.einsum('hrq,ho->orq', hidden.astype(jnp.float32), head_part.astype(jnp.float32)), None)
    delta, unused = lax.scan(add_block, jnp.zeros((OC, NLAT, NLON), jnp.float32), (conv_groups, head_groups))
    ocean_next = (ocean.astype(jnp.float32) + sea_cells[None] * delta).astype(jnp.bfloat16)
    return (atmos_next, grad_atmos, grad_spectral, ocean_next)
```

```python
import math

import jax
import jax.numpy as jnp
from jax import lax
from jax.experimental import pallas as pl
from jax.experimental.pallas import tpu as pltpu
from jax.sharding import PartitionSpec as P

NLAT = 720
NLON = 1024
KMODES = 384
LDEG = 384
ROWS = 90
COLS = 128
CH = 128
OWNERS = 64
SENT = 360
BACK = 368
F32 = jnp.float32
BF16 = jnp.bfloat16
VMEM_LIMIT = 58 * 1024 * 1024


def make_tables(nlat, nlon, kmodes, ldeg):
    column = jnp.arange(nlon, dtype=jnp.int32)[:, None]
    wavenum = jnp.arange(kmodes, dtype=jnp.int32)[None, :]
    phase_cos = (column * wavenum % nlon).astype(jnp.float32) * (2.0 * math.pi / nlon)
    phase_sin = (column * (wavenum + 1) % nlon).astype(jnp.float32) * (2.0 * math.pi / nlon)
    lon_table = (
        jnp.concatenate([jnp.cos(phase_cos), jnp.sin(phase_sin)], axis=1) * math.sqrt(2.0 / nlon)
    ).astype(jnp.bfloat16)
    latrow = jnp.arange(nlat, dtype=jnp.int32)[:, None]
    degree = jnp.arange(ldeg, dtype=jnp.int32)[None, :]
    phase_lat = (degree * (2 * latrow + 1) % (4 * nlat)).astype(jnp.float32) * (
        math.pi / (2 * nlat)
    )
    lat_table = (jnp.cos(phase_lat) * math.sqrt(2.0 / nlat)).astype(jnp.bfloat16)
    return (lon_table, lat_table)


def arrange_lat(lat_table):
    blocks = lat_table.reshape(4, 2, ROWS, LDEG)
    main = blocks[:, :, :80].reshape(4, 160, LDEG)
    middle = blocks[:, :, 80:88].reshape(4, 16, LDEG)
    last = blocks[:, :, None, 88:90]
    made = []
    for m in range(4):
        own = (jnp.arange(4) == m)[None, None, :, None, None]
        tail = jnp.where(own, last, jnp.zeros_like(last)).reshape(4, 16, LDEG)
        made.append(jnp.concatenate([main, middle, tail], axis=1).reshape(768, LDEG))
    return jnp.stack(made)


def pack_kernel(atmos, cotangent, ocean, mask, coupling, out, held_a, held_c, last):
    step = pl.program_id(0)
    gain = jnp.broadcast_to(coupling[...], (CH, COLS)).T
    forcing = mask[...].astype(F32) * ocean[:, 0, :].astype(F32)
    for r in range(16):
        held_a[r * CH : (r + 1) * CH, :] = atmos[r].astype(F32) + forcing[r : r + 1, :] * gain
        held_c[r * CH : (r + 1) * CH, :] = cotangent[r].astype(F32)

    @pl.when(step < 5)
    def _():
        for ch in range(CH):
            for f, held in enumerate((held_a, held_c)):
                at = 32 * f + 16 * (ch % 2)
                out[ch // 2, at : at + 16, :] = held[pl.ds(ch, 16, stride=CH), :].astype(BF16)

    @pl.when(step == 5)
    def _():
        for d in range(OWNERS):
            for f, held in enumerate((held_a, held_c)):
                pair = [held[pl.ds(2 * d + c, 8, stride=CH), :] for c in range(2)]
                out[d, 16 * f : 16 * f + 16, :] = jnp.concatenate(pair, axis=0).astype(BF16)
                for t in range(2):
                    both = held[(8 + t) * CH + 2 * d : (8 + t) * CH + 2 * d + 2, :]
                    for c in range(2):
                        row = 4 * f + 2 * c + t
                        last[row : row + 1, :] = both[c : c + 1]
            out[d, 32:40, :] = last[...].astype(BF16)


def pack(atmos, cotangent, ocean, sea_mask, coupling):
    return pl.pallas_call(
        pack_kernel,
        grid=(6,),
        in_specs=[
            pl.BlockSpec((16, CH, COLS), lambda i: (i, 0, 0)),
            pl.BlockSpec((16, CH, COLS), lambda i: (i, 0, 0)),
            pl.BlockSpec((16, 16, COLS), lambda i: (i, 0, 0)),
            pl.BlockSpec((16, COLS), lambda i: (i, 0)),
            pl.BlockSpec((1, CH), lambda i: (0, 0)),
        ],
        out_specs=pl.BlockSpec((OWNERS, 64, COLS), lambda i: (0, i, 0)),
        out_shape=jax.ShapeDtypeStruct((OWNERS, SENT, COLS), BF16),
        scratch_shapes=[
            pltpu.VMEM((16 * CH, COLS), F32),
            pltpu.VMEM((16 * CH, COLS), F32),
            pltpu.VMEM((8, COLS), F32),
        ],
        compiler_params=pltpu.CompilerParams(vmem_limit_bytes=VMEM_LIMIT),
        name="pack",
    )(atmos, cotangent, ocean, sea_mask, coupling[None, :])


def spectral_kernel(
    got, lon, lon_back, lat, lat_back, weight, out, grad, coef, kept, back, edge_in, edge, halo
):
    step = pl.program_id(0)

    @pl.when(step == 0)
    def _():
        edge_in[...] = jnp.zeros_like(edge_in)
        edge[...] = jnp.zeros_like(edge)

    @pl.when(step < 4)
    def _():
        for n in range(3):
            cols = slice(256 * n, 256 * n + 256)
            found = []
            for a in range(2):
                rows = jnp.concatenate([got[8 * a + o] for o in range(8)], axis=1)
                found.append(jnp.dot(rows, lon[:, cols], preferred_element_type=F32))
            for m in range(4):
                for a in range(2):
                    for i in range(5):
                        coef[m, step, 80 * a + 16 * i : 80 * a + 16 * i + 16, cols] = found[a][
                            64 * i + 16 * m : 64 * i + 16 * m + 16
                        ].astype(BF16)
                coef[m, step, 160:176, cols] = jnp.concatenate(
                    [found[a][320 + 8 * m : 328 + 8 * m] for a in range(2)], axis=0
                ).astype(BF16)
                coef[m, step, 176:192, cols] = jnp.concatenate(
                    [found[a][352:360] for a in range(2)], axis=0
                ).astype(BF16)
        for a in range(2):
            block = 2 * step + a
            for o in range(8):
                lanes = slice(128 * o, 128 * o + 128)
                low = got[8 * a + o, 352:360, :].astype(F32)
                for c in range(2):
                    high = got[8 * a + o, 16 * c : 16 * c + 16, :].astype(F32)
                    edge_in[block + 2, c : c + 1, lanes] = low[2 * c + 1 : 2 * c + 2]
                    edge_in[block, 2 + c : 3 + c, lanes] = high[0:1]

    @pl.when(step == 4)
    def _():
        for c in range(2):
            scale = jnp.concatenate([weight[c], weight[c]], axis=1)
            total = jnp.zeros((LDEG, 128), F32)
            for n in range(3):
                cols = slice(256 * n, 256 * n + 256)
                spectra = []
                for f in range(2):
                    m = 2 * f + c
                    held = coef[m, :, :, cols].reshape(768, 256)
                    found = jnp.dot(lat[m], held, preferred_element_type=F32)
                    kept[m, :, cols] = (found * scale).astype(BF16)
                    spectra.append(found)
                product = spectra[0] * spectra[1]
                total = total + product[:, :128] + product[:, 128:]
            grad[c : c + 1, :] = jnp.sum(total.T, axis=0, keepdims=True) / KMODES
        for n in range(3):
            cols = slice(256 * n, 256 * n + 256)
            tails = [jnp.zeros((16, 256), F32) for _ in range(4)]
            for m in range(4):
                found = jnp.dot(lat_back[m], kept[m, :, cols], preferred_element_type=F32)
                for p in range(4):
                    base = 192 * p
                    back[p, 160 * m : 160 * m + 160, cols] = found[base : base + 160].astype(BF16)
                    back[p, 640 + 16 * m : 656 + 16 * m, cols] = found[
                        base + 160 : base + 176
                    ].astype(BF16)
                    tail = found[base + 176 : base + 192]
                    tails[p] = tails[p] + tail
                    if m < 2:
                        for a in range(2):
                            block = 2 * p + a
                            row = 8 * a + 2 * m + 1
                            edge[block + 2, m : m + 1, cols] = tail[row : row + 1]
                            edge[block, 2 + m : 3 + m, cols] = found[
                                base + 80 * a : base + 80 * a + 1
                            ]
            for p in range(4):
                back[p, 704:720, cols] = tails[p].astype(BF16)
        outside = edge[1:9].reshape(64, 768).astype(BF16)
        halo[...] = (
            jnp.dot(outside, lon_back[...], preferred_element_type=F32)
            + edge_in[1:9].reshape(64, NLON)
        ).reshape(8, 8, NLON)

    @pl.when(step >= 4)
    def _():
        p = step - 4
        rows = back[p]
        for n in range(4):
            cols = slice(256 * n, 256 * n + 256)
            found = jnp.dot(rows, lon_back[:, cols], preferred_element_type=F32)
            for half in range(2):
                o = 2 * n + half
                lanes = slice(128 * half, 128 * half + 128)
                for a in range(2):
                    d = 8 * a + o
                    for i in range(5):
                        for m in range(4):
                            at = 160 * m + 80 * a + 16 * i
                            to = 64 * i + 16 * m
                            out[d, to : to + 16, :] = (
                                found[at : at + 16, lanes] + got[d, to : to + 16, :].astype(F32)
                            ).astype(BF16)
                    for f in range(2):
                        at = 640 + 32 * f + 8 * a
                        to = 320 + 16 * f
                        pair = jnp.concatenate(
                            [found[at : at + 8, lanes], found[at + 16 : at + 24, lanes]], axis=0
                        )
                        out[d, to : to + 16, :] = (
                            pair + got[d, to : to + 16, :].astype(F32)
                        ).astype(BF16)
                    at = 704 + 8 * a
                    low = found[at : at + 8, lanes] + got[d, 352:360, :].astype(F32)
                    beyond = halo[2 * p + a, :, 128 * o : 128 * o + 128]
                    out[d, 352:368, :] = jnp.concatenate([low, beyond], axis=0).astype(BF16)


def spectral(got, lon, lon_back, lat, lat_back, weight):
    once = pl.Buffered(1)
    return pl.pallas_call(
        spectral_kernel,
        grid=(8,),
        in_specs=[
            pl.BlockSpec((16, SENT, COLS), lambda g: (g % 4, 0, 0)),
            pl.BlockSpec((NLON, 768), lambda g: (0, 0), pipeline_mode=once),
            pl.BlockSpec((768, NLON), lambda g: (0, 0), pipeline_mode=once),
            pl.BlockSpec((4, LDEG, 768), lambda g: (0, 0, 0), pipeline_mode=once),
            pl.BlockSpec((4, 768, LDEG), lambda g: (0, 0, 0), pipeline_mode=once),
            pl.BlockSpec((2, LDEG, 128), lambda g: (0, 0, 0), pipeline_mode=once),
        ],
        out_specs=[
            pl.BlockSpec((16, BACK, COLS), lambda g: (jnp.maximum(g - 4, 0), 0, 0)),
            pl.BlockSpec((2, LDEG), lambda g: (0, 0)),
        ],
        out_shape=[
            jax.ShapeDtypeStruct((OWNERS, BACK, COLS), BF16),
            jax.ShapeDtypeStruct((2, LDEG), F32),
        ],
        scratch_shapes=[
            pltpu.VMEM((4, 4, 192, 768), BF16),
            pltpu.VMEM((4, LDEG, 768), BF16),
            pltpu.VMEM((4, 720, 768), BF16),
            pltpu.VMEM((10, 8, NLON), F32),
            pltpu.VMEM((10, 8, 768), F32),
            pltpu.VMEM((8, 8, NLON), F32),
        ],
        compiler_params=pltpu.CompilerParams(vmem_limit_bytes=VMEM_LIMIT),
        cost_estimate=pl.CostEstimate(
            flops=12_500_000_000, bytes_accessed=20_000_000, transcendentals=0
        ),
        name="spectral",
    )(got, lon, lon_back, lat, lat_back, weight)


def spread(main, middle, low, held, field):
    step = pl.program_id(0)

    @pl.when(step < 5)
    def _():
        for ch in range(CH):
            at = 16 * (ch % 2)
            held[pl.ds(ch, 16, stride=CH), :] = main[ch // 2, at : at + 16, :].astype(F32)

    @pl.when(step == 5)
    def _():
        for d in range(OWNERS):
            near = middle[d].astype(F32)
            last = low[d].astype(F32)
            for c in range(2):
                held[pl.ds(2 * d + c, 8, stride=CH), :] = near[8 * c : 8 * c + 8]
                for t in range(2):
                    row = 4 * field + 2 * c + t
                    at = (8 + t) * CH + 2 * d + c
                    held[at : at + 1, :] = last[row : row + 1]


def unpack_flux_kernel(main, middle, low, weight, out, flux, held, outside):
    step = pl.program_id(0)
    spread(main, middle, low, held, 0)
    out[...] = held[...].reshape(16, CH, COLS).astype(BF16)

    def put(row, cells):
        found = jnp.dot(weight[...], cells, preferred_element_type=F32)
        flux[row] = found[0:4].astype(BF16)

    @pl.when(step < 5)
    def _():
        for r in range(16):
            put(1 + 16 * step + r, out[r])

    @pl.when(step == 5)
    def _():
        for r in range(10):
            put(81 + r, out[r])
        for d in range(OWNERS):
            beyond = low[d].astype(F32)
            for side in range(2):
                outside[side, 2 * d : 2 * d + 2, :] = beyond[8 + 2 * side : 10 + 2 * side]
        put(0, outside[0].astype(BF16))
        put(91, outside[1].astype(BF16))


def unpack_kernel(main, middle, low, out, held):
    spread(main, middle, low, held, 1)
    out[...] = held[...].reshape(16, CH, COLS).astype(BF16)


def unpack_specs(field):
    return [
        pl.BlockSpec((OWNERS, 32, COLS), lambda i: (0, 2 * jnp.minimum(i, 4) + field, 0)),
        pl.BlockSpec((OWNERS, 16, COLS), lambda i: (0, 20 + field, 0)),
        pl.BlockSpec((OWNERS, 16, COLS), lambda i: (0, 22, 0)),
    ]


def unpack_flux(sent_back, weight):
    return pl.pallas_call(
        unpack_flux_kernel,
        grid=(6,),
        in_specs=unpack_specs(0) + [pl.BlockSpec((16, CH), lambda i: (0, 0))],
        out_specs=[
            pl.BlockSpec((16, CH, COLS), lambda i: (i, 0, 0)),
            pl.BlockSpec((ROWS + 2, 4, COLS), lambda i: (0, 0, 0)),
        ],
        out_shape=[
            jax.ShapeDtypeStruct((ROWS, CH, COLS), BF16),
            jax.ShapeDtypeStruct((ROWS + 2, 4, COLS), BF16),
        ],
        scratch_shapes=[pltpu.VMEM((16 * CH, COLS), F32), pltpu.VMEM((2, CH, COLS), F32)],
        compiler_params=pltpu.CompilerParams(vmem_limit_bytes=VMEM_LIMIT),
        name="unpack_flux",
    )(sent_back, sent_back, sent_back, weight)


def unpack(sent_back):
    return pl.pallas_call(
        unpack_kernel,
        grid=(6,),
        in_specs=unpack_specs(1),
        out_specs=pl.BlockSpec((16, CH, COLS), lambda i: (i, 0, 0)),
        out_shape=jax.ShapeDtypeStruct((ROWS, CH, COLS), BF16),
        scratch_shapes=[pltpu.VMEM((16 * CH, COLS), F32)],
        compiler_params=pltpu.CompilerParams(vmem_limit_bytes=VMEM_LIMIT),
        cost_estimate=pl.CostEstimate(flops=0, bytes_accessed=6_000_000, transcendentals=0),
        name="unpack",
    )(sent_back, sent_back, sent_back)


def ocean_kernel(
    taps, more, own, other, left, left_other, right, right_other, conv, head, ocean, mask, out, fluxes
):
    step = pl.program_id(0)

    @pl.when(step == 0)
    def _():
        def whole(one, two):
            total = one[...].astype(F32) + two[...].astype(F32)
            return total.astype(BF16).astype(F32)

        lane = lax.broadcasted_iota(jnp.int32, (ROWS + 2, 4, COLS), 2)
        middle = whole(own, other)
        west = whole(left, left_other)
        east = whole(right, right_other)
        fluxes[:, 0:4, :] = jnp.where(
            lane == 0, pltpu.roll(west, 1, 2), pltpu.roll(middle, 1, 2)
        )
        fluxes[:, 4:8, :] = middle
        fluxes[:, 8:12, :] = jnp.where(
            lane == COLS - 1, pltpu.roll(east, COLS - 1, 2), pltpu.roll(middle, COLS - 1, 2)
        )
        fluxes[:, 12:16, :] = jnp.zeros((ROWS + 2, 4, COLS), F32)

    def cells(row):
        known = taps[row, 0:240, :] if row < 10 else more[row - 10, 0:240, :]
        return jnp.concatenate([known, fluxes[10 * step + row].astype(BF16)], axis=0)

    for pair in range(5):
        rows = [cells(2 * pair + k) for k in range(4)]
        around = jnp.concatenate(
            [jnp.concatenate(rows[0:3], axis=0), jnp.concatenate(rows[1:4], axis=0)], axis=1
        )
        summed = jnp.dot(conv[...], around, preferred_element_type=F32)
        hidden = jax.nn.gelu(summed).astype(BF16)
        delta = jnp.dot(head[...], hidden, preferred_element_type=F32)
        for k in range(2):
            row = 2 * pair + k
            sea = mask[pl.ds(10 * step + row, 1), :].astype(F32)
            out[row] = (
                ocean[row].astype(F32) + sea * delta[0:76, COLS * k : COLS * k + COLS]
            ).astype(BF16)


def ocean_step(taps, fluxes, conv, head, ocean, sea_mask):
    flux_spec = pl.BlockSpec((ROWS + 2, 4, COLS), lambda g: (0, 0, 0))
    return pl.pallas_call(
        ocean_kernel,
        grid=(9,),
        in_specs=[
            pl.BlockSpec((10, 256, COLS), lambda g: (g, 0, 0)),
            pl.BlockSpec((2, 256, COLS), lambda g: (5 * g + 5, 0, 0)),
        ]
        + [flux_spec] * 6
        + [
            pl.BlockSpec((256, 768), lambda g: (0, 0)),
            pl.BlockSpec((80, 256), lambda g: (0, 0)),
            pl.BlockSpec((10, 76, COLS), lambda g: (g, 0, 0)),
            pl.BlockSpec((ROWS, COLS), lambda g: (0, 0)),
        ],
        out_specs=pl.BlockSpec((10, 76, COLS), lambda g: (g, 0, 0)),
        out_shape=jax.ShapeDtypeStruct((ROWS, 76, COLS), BF16),
        scratch_shapes=[pltpu.VMEM((ROWS + 2, 16, COLS), F32)],
        compiler_params=pltpu.CompilerParams(vmem_limit_bytes=VMEM_LIMIT),
        name="ocean",
    )(taps, taps, *fluxes, conv, head, ocean, sea_mask)


def after(value, *others):
    return lax.optimization_barrier((value,) + others)[0]


def local(
    atmos,
    cotangent,
    ocean,
    sea_mask,
    spectral_weight,
    coupling,
    flux_weight,
    conv_weight,
    head_weight,
):
    atmos = atmos.transpose(1, 0, 2)
    cotangent = cotangent.transpose(1, 0, 2)
    ocean = ocean.transpose(1, 0, 2)
    ring = range(8)
    east = [(k, (k + 1) % 8) for k in ring]
    west = [((k + 1) % 8, k) for k in ring]
    swap = [(0, 1), (1, 0)]

    sent = pack(atmos, cotangent, ocean, sea_mask, coupling)
    got = lax.all_to_all(sent, ("lat", "lon"), split_axis=0, concat_axis=0, tiled=True)

    lon_table, lat_table = make_tables(NLAT, NLON, KMODES, LDEG)
    lat_back = arrange_lat(lat_table)
    lat = lat_back.transpose(0, 2, 1)
    scale = jnp.broadcast_to(spectral_weight[:, :, None], (2, LDEG, 128))
    hidden_weights = jnp.concatenate(
        [conv_weight.reshape(720, 128), head_weight.T], axis=0
    )
    hidden_weights = after(hidden_weights, sent)
    weights = jnp.concatenate(
        [hidden_weights, lax.ppermute(hidden_weights, "group", swap)], axis=1
    )
    below = after(ocean[ROWS - 1 :], sent)
    above = after(ocean[:1], sent)
    top = lax.ppermute(below, "lat", [(k, k + 1) for k in range(7)])
    bottom = lax.ppermute(above, "lat", [(k + 1, k) for k in range(7)])
    conv = weights[:720].reshape(3, 3, 80, 256)
    conv = jnp.concatenate(
        [
            conv[:, :, :76].reshape(3, 3, 76, 256),
            jnp.zeros((3, 3, 4, 256), BF16),
        ],
        axis=2,
    ).reshape(3, 240, 256)
    conv_flux = weights[:720].reshape(3, 3, 80, 256)[:, :, 76:].reshape(3, 12, 256)
    conv = jnp.concatenate([conv, conv_flux, jnp.zeros((3, 4, 256), BF16)], axis=1)
    conv = conv.reshape(768, 256).T
    head = jnp.concatenate([weights[720:], jnp.zeros((4, 256), BF16)], axis=0)
    flux_rows = jnp.concatenate([flux_weight, jnp.zeros((12, CH), BF16)], axis=0)

    sent_back, grad_spectral = spectral(got, lon_table, lon_table.T, lat, lat_back, scale)
    returned = lax.all_to_all(sent_back, ("lat", "lon"), split_axis=0, concat_axis=0, tiled=True)

    tall = after(jnp.concatenate([top, ocean, bottom], axis=0), sent_back)
    first = lax.ppermute(tall[:, :, COLS - 1], "lon", east)[:, :, None]
    final = lax.ppermute(tall[:, :, 0], "lon", west)[:, :, None]
    wide = jnp.concatenate([first, tall, final], axis=2)
    taps = jnp.stack([wide[:, :, b : b + COLS] for b in range(3)], axis=1)
    taps = jnp.pad(taps, ((0, 8), (0, 0), (0, 4), (0, 0))).reshape(100, 240, COLS)
    taps = jnp.pad(taps, ((0, 0), (0, 16), (0, 0)))

    atmos_next, flux = unpack_flux(returned, flux_rows)
    across = [(8 * g + k, 8 * (1 - g) + (k + 1) % 8) for g in range(2) for k in ring]
    counter = [(8 * g + k, 8 * (1 - g) + (k - 1) % 8) for g in range(2) for k in ring]
    fluxes = [
        flux,
        lax.ppermute(flux, "group", swap),
        lax.ppermute(flux, "lon", east),
        lax.ppermute(flux, ("group", "lon"), across),
        lax.ppermute(flux, "lon", west),
        lax.ppermute(flux, ("group", "lon"), counter),
    ]
    grad_atmos = unpack(after(returned, flux))
    ocean_next = ocean_step(taps, fluxes, conv, head, ocean, sea_mask)
    return (
        atmos_next.transpose(1, 0, 2),
        grad_atmos.transpose(1, 0, 2),
        grad_spectral,
        ocean_next.transpose(1, 0, 2),
    )


def solution(mesh):
    in_specs = (
        P("group", "lat", "lon"),
        P("group", "lat", "lon"),
        P(None, "lat", "lon"),
        P("lat", "lon"),
        P(("group", "lat", "lon"), None),
        P("group"),
        P(None, "group"),
        P(None, None, None, "group"),
        P("group", None),
    )
    out_specs = (
        P("group", "lat", "lon"),
        P("group", "lat", "lon"),
        P(("group", "lat", "lon"), None),
        P(None, "lat", "lon"),
    )
    return jax.shard_map(local, mesh=mesh, in_specs=in_specs, out_specs=out_specs, check_vma=False)
```

```python
import math

import jax
import jax.numpy as jnp
import ml_dtypes
import numpy as np
from jax import lax
from jax.experimental import pallas as pl
from jax.experimental.pallas import tpu as pltpu
from jax.sharding import PartitionSpec as P

NLAT = 720
NLON = 1024
KMODES = 384
LDEG = 384
ROWS = 90
COLS = 128
CH = 128
OWNERS = 64
SENT = 360
BACK = 368
PITCH = CH + 1
F32 = jnp.float32
BF16 = jnp.bfloat16
MIB = 1024 * 1024
GELU_ONE = math.sqrt(2.0 / math.pi)
GELU_THREE = 0.044715 * GELU_ONE


def make_tables(nlat, nlon, kmodes, ldeg):
    column = np.arange(nlon, dtype=np.int64)[:, None]
    wavenum = np.arange(kmodes, dtype=np.int64)[None, :]
    step = np.float32(2.0 * math.pi / nlon)
    phase_cos = (column * wavenum % nlon).astype(np.float32) * step
    phase_sin = (column * (wavenum + 1) % nlon).astype(np.float32) * step
    lon_table = np.concatenate([np.cos(phase_cos), np.sin(phase_sin)], axis=1)
    lon_table = lon_table * np.float32(math.sqrt(2.0 / nlon))
    latrow = np.arange(nlat, dtype=np.int64)[:, None]
    degree = np.arange(ldeg, dtype=np.int64)[None, :]
    phase_lat = (degree * (2 * latrow + 1) % (4 * nlat)).astype(np.float32) * np.float32(
        math.pi / (2 * nlat)
    )
    lat_table = np.cos(phase_lat) * np.float32(math.sqrt(2.0 / nlat))
    return (lon_table.astype(ml_dtypes.bfloat16), lat_table.astype(ml_dtypes.bfloat16))


def arrange_lon(lon_table):
    cosines = np.arange(KMODES)
    sines = np.arange(1, KMODES + 1)
    place = np.concatenate([cosines, sines])
    zero = lon_table[:256, place % 4 == 0]
    two = lon_table[:256, place % 4 == 2]
    odd = lon_table[:512, place % 2 == 1]
    blank = np.zeros((256, 64), lon_table.dtype)
    return (
        np.concatenate([zero, blank], axis=1),
        np.concatenate([blank, two], axis=1),
        odd,
    )


def arrange_lat(lat_table):
    blocks = lat_table.reshape(4, 2, ROWS, LDEG)
    main = blocks[:, :, :80].reshape(4, 160, LDEG)
    middle = blocks[:, :, 80:88].reshape(4, 16, LDEG)
    last = blocks[:, :, 88:90]
    made = []
    for m in range(4):
        tail = np.zeros((4, 2, 4, 2, LDEG), lat_table.dtype)
        tail[:, :, m] = last
        tail = tail.reshape(4, 16, LDEG)
        made.append(np.concatenate([main, middle, tail], axis=1).reshape(768, LDEG))
    return np.stack(made)


def pack_kernel(
    atmos,
    cotangent,
    ocean,
    mask,
    coupling,
    conv,
    head,
    out,
    weights,
    below,
    above,
    in_a,
    in_c,
    warm,
    sea_cells,
    gains,
    decoder,
    held_a,
    held_c,
    last,
    sems,
):
    def fetches(i, rows):
        span = pl.ds(16 * i, rows)
        return [
            pltpu.make_async_copy(atmos.at[span], in_a.at[span], sems.at[0, i]),
            pltpu.make_async_copy(cotangent.at[span], in_c.at[span], sems.at[1, i]),
        ]

    surface = [
        pltpu.make_async_copy(ocean.at[:, pl.ds(0, 16), :], warm, sems.at[2, 0]),
        pltpu.make_async_copy(mask, sea_cells, sems.at[2, 1]),
        pltpu.make_async_copy(coupling, gains, sems.at[2, 2]),
    ]
    others = [
        pltpu.make_async_copy(conv, weights.at[pl.ds(0, 720)], sems.at[2, 3]),
        pltpu.make_async_copy(head, decoder, sems.at[2, 4]),
        pltpu.make_async_copy(ocean.at[pl.ds(ROWS - 1, 1)], below, sems.at[2, 5]),
        pltpu.make_async_copy(ocean.at[pl.ds(0, 1)], above, sems.at[3, 0]),
    ]
    for copy in surface:
        copy.start()
    for i in range(6):
        for copy in fetches(i, 16 if i < 5 else 10):
            copy.start()
    for copy in others:
        copy.start()
    for copy in surface:
        copy.wait()
    gain = jnp.broadcast_to(gains[...], (CH, COLS)).T

    def widen(i, rows):
        for copy in fetches(i, rows):
            copy.wait()
        for r in range(rows):
            row = 16 * i + r
            sea = sea_cells[pl.ds(row, 1), :].astype(F32)
            forcing = sea * warm[row].astype(F32)[0:1]
            held_a[r * PITCH : r * PITCH + CH, :] = in_a[row].astype(F32) + forcing * gain
            held_c[r * PITCH : r * PITCH + CH, :] = in_c[row].astype(F32)

    @pl.loop(0, 5)
    def _(i):
        widen(i, 16)
        base = pl.multiple_of(64 * i, 64)
        for ch in range(CH):
            for f, held in enumerate((held_a, held_c)):
                at = base + 32 * f + 16 * (ch % 2)
                out[ch // 2, pl.ds(at, 16), :] = held[pl.ds(ch, 16, stride=PITCH), :].astype(BF16)

    widen(5, 10)
    for d in range(OWNERS):
        for f, held in enumerate((held_a, held_c)):
            pair = [held[pl.ds(2 * d + c, 8, stride=PITCH), :] for c in range(2)]
            out[d, 320 + 16 * f : 336 + 16 * f, :] = jnp.concatenate(pair, axis=0).astype(BF16)
            for t in range(2):
                both = held[(8 + t) * PITCH + 2 * d : (8 + t) * PITCH + 2 * d + 2, :]
                for c in range(2):
                    row = 4 * f + 2 * c + t
                    last[d, row : row + 1, :] = both[c : c + 1]
        out[d, 352:360, :] = last[d].astype(BF16)

    for copy in others:
        copy.wait()
    weights[720:800, :] = jnp.concatenate(
        [decoder[...].astype(F32), jnp.zeros((4, 128), F32)], axis=0
    ).astype(BF16)


def vmem():
    return pl.BlockSpec(memory_space=pltpu.VMEM)


def near(array):
    return pltpu.with_memory_space_constraint(array, pltpu.VMEM)


def in_hbm():
    return pl.BlockSpec(memory_space=pltpu.HBM)


def pack(atmos, cotangent, ocean, sea_mask, coupling, conv, head):
    given = (atmos, cotangent, ocean, sea_mask, coupling[None, :], conv, head)
    return pl.pallas_call(
        pack_kernel,
        in_specs=[in_hbm()] * 7,
        out_specs=[vmem()] * 4,
        out_shape=[
            pltpu.VMEM((OWNERS, SENT, COLS), BF16),
            pltpu.VMEM((800, 128), BF16),
            pltpu.VMEM((1, 76, COLS), BF16),
            pltpu.VMEM((1, 76, COLS), BF16),
        ],
        scratch_shapes=[
            pltpu.VMEM((ROWS, CH, COLS), BF16),
            pltpu.VMEM((ROWS, CH, COLS), BF16),
            pltpu.VMEM((ROWS, 16, COLS), BF16),
            pltpu.VMEM((ROWS, COLS), jnp.int32),
            pltpu.VMEM((1, CH), F32),
            pltpu.VMEM((76, 128), BF16),
            pltpu.VMEM((16 * PITCH, COLS), F32),
            pltpu.VMEM((16 * PITCH, COLS), F32),
            pltpu.VMEM((OWNERS, 8, COLS), F32),
            pltpu.SemaphoreType.DMA((4, 6)),
        ],
        compiler_params=pltpu.CompilerParams(vmem_limit_bytes=14 * MIB),
        name="pack",
    )(*[pltpu.with_memory_space_constraint(array, pltpu.HBM) for array in given])


def spectral_kernel(
    got,
    lon_zero,
    lon_two,
    lon_odd,
    back_zero,
    back_two,
    back_odd,
    lat,
    lat_back,
    weight,
    out,
    grad,
    coef,
    kept,
    back,
    edge_in,
    edge,
    halo,
):
    edge_in[...] = jnp.zeros_like(edge_in)
    edge[...] = jnp.zeros_like(edge)

    def dot(one, two):
        return jnp.dot(one, two, preferred_element_type=F32)

    @pl.loop(0, 4)
    def _(p):
        found = []
        for a in range(2):
            first = 16 * p + 8 * a
            quarter = [
                jnp.concatenate([got[first + 2 * q + h].astype(F32) for h in range(2)], axis=1)
                for q in range(4)
            ]
            even_0 = quarter[0] + quarter[2]
            even_1 = quarter[1] + quarter[3]
            odd = jnp.concatenate(
                [(quarter[0] - quarter[2]).astype(BF16), (quarter[1] - quarter[3]).astype(BF16)],
                axis=1,
            )
            zero = dot((even_0 + even_1).astype(BF16), lon_zero[...])
            two = dot((even_0 - even_1).astype(BF16), lon_two[...])
            found.append(
                [
                    zero[:, 0:128],
                    zero[:, 128:256] + two[:, 0:128],
                    two[:, 128:256],
                    dot(odd, lon_odd[...]),
                ]
            )
        for n, cols in enumerate(
            (slice(0, 128), slice(128, 256), slice(256, 384), slice(384, 768))
        ):
            for m in range(4):
                for a in range(2):
                    for i in range(5):
                        coef[m, p, 80 * a + 16 * i : 80 * a + 16 * i + 16, cols] = found[a][n][
                            64 * i + 16 * m : 64 * i + 16 * m + 16
                        ].astype(BF16)
                coef[m, p, 160:176, cols] = jnp.concatenate(
                    [found[a][n][320 + 8 * m : 328 + 8 * m] for a in range(2)], axis=0
                ).astype(BF16)
                coef[m, p, 176:192, cols] = jnp.concatenate(
                    [found[a][n][352:360] for a in range(2)], axis=0
                ).astype(BF16)
        for a in range(2):
            block = 2 * p + a
            for o in range(8):
                lanes = slice(128 * o, 128 * o + 128)
                low = got[8 * block + o, 352:360, :].astype(F32)
                for c in range(2):
                    high = got[8 * block + o, 16 * c : 16 * c + 16, :].astype(F32)
                    edge_in[block + 2, c : c + 1, lanes] = low[2 * c + 1 : 2 * c + 2]
                    edge_in[block, 2 + c : 3 + c, lanes] = high[0:1]

    for c in range(2):
        scale = jnp.broadcast_to(weight[c : c + 1, :], (256, LDEG)).T
        total = jnp.zeros((LDEG, 128), F32)
        for n in range(3):
            cols = slice(256 * n, 256 * n + 256)
            spectra = []
            for f in range(2):
                m = 2 * f + c
                found = dot(lat[m], coef[m, :, :, cols].reshape(768, 256))
                kept[m, :, cols] = (found * scale).astype(BF16)
                spectra.append(found)
            product = spectra[0] * spectra[1]
            total = total + product[:, :128] + product[:, 128:]
        grad[c : c + 1, :] = jnp.sum(total.T, axis=0, keepdims=True) / KMODES
    for n in range(3):
        cols = slice(256 * n, 256 * n + 256)
        tails = [jnp.zeros((16, 256), F32) for _ in range(4)]
        for m in range(4):
            found = dot(lat_back[m], kept[m, :, cols])
            for p in range(4):
                base = 192 * p
                back[p, 160 * m : 160 * m + 160, cols] = found[base : base + 160].astype(BF16)
                back[p, 640 + 16 * m : 656 + 16 * m, cols] = found[
                    base + 160 : base + 176
                ].astype(BF16)
                tail = found[base + 176 : base + 192]
                tails[p] = tails[p] + tail
                if m < 2:
                    for a in range(2):
                        block = 2 * p + a
                        row = 8 * a + 2 * m + 1
                        edge[block + 2, m : m + 1, cols] = tail[row : row + 1]
                        edge[block, 2 + m : 3 + m, cols] = found[base + 80 * a : base + 80 * a + 1]
        for p in range(4):
            back[p, 704:720, cols] = tails[p].astype(BF16)

    def inverse(rows):
        zero = dot(rows[:, 0:256], back_zero[...])
        two = dot(rows[:, 128:384], back_two[...])
        for n in range(2):
            even = zero + two if n == 0 else zero - two
            odd = dot(rows[:, 384:768], back_odd[:, 256 * n : 256 * n + 256])
            yield 2 * n, even + odd
            yield 2 * n + 4, even - odd

    for o, found in inverse(edge[1:9].reshape(64, 768).astype(BF16)):
        lanes = slice(128 * o, 128 * o + 256)
        halo[:, :, lanes] = found.reshape(8, 8, 256) + edge_in[1:9, :, lanes]

    @pl.loop(0, 4)
    def _(p):
        for first, found in inverse(back[p]):
            for half in range(2):
                o = first + half
                lanes = slice(128 * half, 128 * half + 128)
                for a in range(2):
                    d = 16 * p + 8 * a + o
                    for i in range(5):
                        for m in range(4):
                            at = 160 * m + 80 * a + 16 * i
                            to = 64 * i + 16 * m
                            out[d, to : to + 16, :] = (
                                found[at : at + 16, lanes] + got[d, to : to + 16, :].astype(F32)
                            ).astype(BF16)
                    for f in range(2):
                        at = 640 + 32 * f + 8 * a
                        to = 320 + 16 * f
                        pair = jnp.concatenate(
                            [found[at : at + 8, lanes], found[at + 16 : at + 24, lanes]], axis=0
                        )
                        out[d, to : to + 16, :] = (
                            pair + got[d, to : to + 16, :].astype(F32)
                        ).astype(BF16)
                    at = 704 + 8 * a
                    low = found[at : at + 8, lanes] + got[d, 352:360, :].astype(F32)
                    beyond = halo[2 * p + a, :, 128 * o : 128 * o + 128]
                    out[d, 352:368, :] = jnp.concatenate([low, beyond], axis=0).astype(BF16)


def spectral(got, lon, lat, weight):
    tables = list(lon) + [table.T for table in lon] + [lat.transpose(0, 2, 1), lat]
    return pl.pallas_call(
        spectral_kernel,
        in_specs=[vmem()] * 10,
        out_specs=[vmem(), vmem()],
        out_shape=[
            pltpu.VMEM((OWNERS, BACK, COLS), BF16),
            jax.ShapeDtypeStruct((2, LDEG), F32),
        ],
        scratch_shapes=[
            pltpu.VMEM((4, 4, 192, 768), BF16),
            pltpu.VMEM((4, LDEG, 768), BF16),
            pltpu.VMEM((4, 720, 768), BF16),
            pltpu.VMEM((10, 8, NLON), F32),
            pltpu.VMEM((10, 8, 768), F32),
            pltpu.VMEM((8, 8, NLON), F32),
        ],
        compiler_params=pltpu.CompilerParams(vmem_limit_bytes=20 * MIB),
        name="spectral",
    )(near(got), *[near(jnp.asarray(np.ascontiguousarray(table))) for table in tables], weight)


def spread(sent_back, i, field, held):
    base = pl.multiple_of(64 * i, 64) + 32 * field
    for ch in range(CH):
        at = base + 16 * (ch % 2)
        held[pl.ds(ch, 16, stride=PITCH), :] = sent_back[ch // 2, pl.ds(at, 16), :].astype(F32)


def spread_last(sent_back, field, held):
    for d in range(OWNERS):
        near = sent_back[d, 320 + 16 * field : 336 + 16 * field, :].astype(F32)
        last = sent_back[d, 352:368, :].astype(F32)
        for c in range(2):
            held[pl.ds(2 * d + c, 8, stride=PITCH), :] = near[8 * c : 8 * c + 8]
            for t in range(2):
                row = 4 * field + 2 * c + t
                at = (8 + t) * PITCH + 2 * d + c
                held[at : at + 1, :] = last[row : row + 1]


def unpack_rows(sent_back, field, out, held, staged, sems, visit):
    def send(i, rows):
        span = pl.ds(16 * i, rows)
        return pltpu.make_async_copy(staged.at[span], out.at[span], sems.at[i])

    @pl.loop(0, 5)
    def _(i):
        spread(sent_back, i, field, held)
        for r in range(16):
            staged[16 * i + r] = held[r * PITCH : r * PITCH + CH, :].astype(BF16)
            visit(16 * i + r)
        send(i, 16).start()

    spread_last(sent_back, field, held)
    for r in range(10):
        staged[80 + r] = held[r * PITCH : r * PITCH + CH, :].astype(BF16)
        visit(80 + r)
    send(5, 10).start()

    def finish():
        for i in range(6):
            send(i, 16 if i < 5 else 10).wait()

    return finish


def unpack_flux_kernel(
    sent_back,
    weight,
    ocean,
    top,
    bottom,
    out,
    flux,
    to_east,
    to_west,
    held,
    staged,
    outside,
    found,
    sems,
):
    def put(row, cells):
        sums = jnp.dot(weight[...], cells, preferred_element_type=F32)
        found[pl.ds(4 * row, 4), :] = sums[0:4]

    finish = unpack_rows(
        sent_back, 0, out, held, staged, sems, lambda row: put(row + 1, staged[row])
    )
    for d in range(OWNERS):
        beyond = sent_back[d, 352:368, :].astype(F32)
        for side in range(2):
            outside[side, 2 * d : 2 * d + 2, :] = beyond[8 + 2 * side : 10 + 2 * side]
    put(0, outside[0].astype(BF16))
    put(91, outside[1].astype(BF16))

    lane = lax.broadcasted_iota(jnp.int32, (76, COLS), 1)

    def gather(row, cells, kept):
        at = lane == row
        return (
            jnp.where(at, pltpu.roll(cells, lax.rem(row + 1, COLS), 1), kept[0]),
            jnp.where(at, pltpu.roll(cells, row, 1), kept[1]),
        )

    blank = jnp.zeros((76, COLS), BF16)
    edges = gather(jnp.int32(0), top[0], (blank, blank))
    edges = gather(jnp.int32(91), bottom[0], edges)
    edges = lax.fori_loop(
        0, ROWS, lambda row, kept: gather(row + 1, ocean[row], kept), edges, unroll=18
    )

    sums = found[...].astype(BF16)
    flux[...] = sums
    for side, message in enumerate((to_east, to_west)):
        message[0:368, :] = sums
        message[368:448, :] = jnp.concatenate(
            [edges[side].astype(F32), jnp.zeros((4, COLS), F32)], axis=0
        ).astype(BF16)
    finish()


def unpack_taps_kernel(
    sent_back,
    weights,
    weights_other,
    ocean,
    top,
    bottom,
    out,
    taps,
    conv,
    head,
    held,
    staged,
    sems,
):
    finish = unpack_rows(sent_back, 1, out, held, staged, sems, lambda row: None)

    for half, given in enumerate((weights, weights_other)):
        rows = slice(128 * half, 128 * half + 128)
        wide = jnp.concatenate([given[0:720, :].astype(F32), jnp.zeros((48, 128), F32)], axis=0)
        conv[rows, :] = wide.T.astype(BF16)
        head[:, rows] = given[720:800, :]

    def build(row, cells):
        wide = jnp.concatenate([cells, jnp.zeros((4, COLS), BF16)], axis=0)
        base = pl.multiple_of(240 * row, 16)
        taps[pl.ds(base, 80), :] = pltpu.roll(wide, 1, 1)
        taps[pl.ds(base + 80, 80), :] = wide
        taps[pl.ds(base + 160, 80), :] = pltpu.roll(wide, COLS - 1, 1)

    build(0, top[0])
    build(91, bottom[0])
    taps[92 * 240 :, :] = jnp.zeros((48, COLS), BF16)

    @pl.loop(0, ROWS, unroll=18)
    def _(row):
        build(row + 1, ocean[row])

    finish()


def unpack_scratch():
    return [pltpu.VMEM((16 * PITCH, COLS), F32), pltpu.VMEM((ROWS, CH, COLS), BF16)]


def unpack_flux(sent_back, weight, ocean, top, bottom):
    return pl.pallas_call(
        unpack_flux_kernel,
        in_specs=[vmem()] * 5,
        out_specs=[in_hbm(), vmem(), vmem(), vmem()],
        out_shape=[
            jax.ShapeDtypeStruct((ROWS, CH, COLS), BF16),
            jax.ShapeDtypeStruct((368, COLS), BF16),
            jax.ShapeDtypeStruct((448, COLS), BF16),
            jax.ShapeDtypeStruct((448, COLS), BF16),
        ],
        scratch_shapes=unpack_scratch()
        + [
            pltpu.VMEM((2, CH, COLS), F32),
            pltpu.VMEM((368, COLS), F32),
            pltpu.SemaphoreType.DMA((6,)),
        ],
        compiler_params=pltpu.CompilerParams(vmem_limit_bytes=12 * MIB),
        name="unpack_flux",
    )(near(sent_back), weight, near(ocean), top, bottom)


def unpack_taps(sent_back, weights, weights_other, ocean, top, bottom):
    return pl.pallas_call(
        unpack_taps_kernel,
        in_specs=[vmem()] * 6,
        out_specs=[in_hbm(), vmem(), vmem(), vmem()],
        out_shape=[
            jax.ShapeDtypeStruct((ROWS, CH, COLS), BF16),
            pltpu.VMEM((92 * 240 + 48, COLS), BF16),
            pltpu.VMEM((256, 768), BF16),
            pltpu.VMEM((80, 256), BF16),
        ],
        scratch_shapes=unpack_scratch() + [pltpu.SemaphoreType.DMA((6,))],
        compiler_params=pltpu.CompilerParams(vmem_limit_bytes=12 * MIB),
        cost_estimate=pl.CostEstimate(flops=0, bytes_accessed=12_000_000, transcendentals=0),
        name="unpack_taps",
    )(near(sent_back), weights, weights_other, near(ocean), top, bottom)


def ocean_kernel(
    own,
    other,
    left,
    left_other,
    right,
    right_other,
    unfinished,
    conv,
    head,
    ocean,
    mask,
    out,
    taps,
    fluxes,
    hidden,
    staged,
    sems,
):
    def whole(one, two):
        total = one[0:368, :].astype(F32) + two[...].astype(F32)
        return total.astype(BF16).astype(F32)

    column = lax.broadcasted_iota(jnp.int32, (368, COLS), 1)
    middle = whole(own, other)
    west = pltpu.roll(whole(left, left_other), 1, 1)
    east = pltpu.roll(whole(right, right_other), COLS - 1, 1)
    fluxes[0] = jnp.where(column == 0, west, pltpu.roll(middle, 1, 1))
    fluxes[1] = middle
    fluxes[2] = jnp.where(column == COLS - 1, east, pltpu.roll(middle, COLS - 1, 1))

    lane = lax.broadcasted_iota(jnp.int32, (80, COLS), 1)
    first_edge = left[368:448, :]
    final_edge = right[368:448, :]

    taps[92 * 240 :, :] = jnp.zeros((48, COLS), BF16)

    @pl.loop(0, ROWS + 2, unroll=23)
    def _(row):
        base = pl.multiple_of(240 * row, 16)
        first = pltpu.roll(first_edge, lax.rem(COLS - row, COLS), 1)
        final = pltpu.roll(final_edge, COLS - 1 - row, 1)
        shifts = (
            jnp.where(lane == 0, first, unfinished[pl.ds(base, 80), :]),
            unfinished[pl.ds(base + 80, 80), :],
            jnp.where(lane == COLS - 1, final, unfinished[pl.ds(base + 160, 80), :]),
        )
        for b, cells in enumerate(shifts):
            at = base + 80 * b
            taps[pl.ds(at, 64), :] = cells[0:64]
            rest = [cells[64:80].astype(F32)[0:12], fluxes[b, pl.ds(4 * row, 4), :]]
            taps[pl.ds(at + 64, 16), :] = jnp.concatenate(rest, axis=0).astype(BF16)

    def send(g):
        span = pl.ds(10 * g, 10)
        return pltpu.make_async_copy(staged.at[span], out.at[span], sems.at[g])

    def window(row):
        return taps[pl.ds(pl.multiple_of(240 * row, 16), 768), :]

    def convolve(g):
        for pair in range(5):
            first = 10 * g + 2 * pair
            around = jnp.concatenate([window(first), window(first + 1)], axis=1)
            x = jnp.dot(conv[...], around, preferred_element_type=F32)
            bent = jnp.tanh(x * (GELU_ONE + GELU_THREE * (x * x)))
            half = 0.5 * x
            hidden[lax.rem(g, 2), :, 256 * pair : 256 * pair + 256] = (half + half * bent).astype(
                BF16
            )

    def decode(g):
        delta = jnp.dot(head[...], hidden[lax.rem(g, 2)], preferred_element_type=F32)
        for k in range(10):
            row = 10 * g + k
            sea = mask[pl.ds(row, 1), :].astype(F32)
            staged[row] = (
                ocean[row].astype(F32) + sea * delta[0:76, COLS * k : COLS * k + COLS]
            ).astype(BF16)
        send(g).start()

    convolve(jnp.int32(0))

    @pl.loop(1, 9)
    def _(g):
        convolve(g)
        decode(g - 1)

    decode(jnp.int32(8))
    for g in range(9):
        send(g).wait()


def ocean_step(fluxes, taps, conv, head, ocean, sea_mask):
    return pl.pallas_call(
        ocean_kernel,
        in_specs=[vmem()] * 11,
        out_specs=in_hbm(),
        out_shape=jax.ShapeDtypeStruct((ROWS, 76, COLS), BF16),
        scratch_shapes=[
            pltpu.VMEM((92 * 240 + 48, COLS), BF16),
            pltpu.VMEM((3, 368, COLS), F32),
            pltpu.VMEM((2, 256, 1280), BF16),
            pltpu.VMEM((ROWS, 76, COLS), BF16),
            pltpu.SemaphoreType.DMA((9,)),
        ],
        compiler_params=pltpu.CompilerParams(vmem_limit_bytes=14 * MIB),
        name="ocean",
    )(*fluxes, near(taps), near(conv), near(head), near(ocean), sea_mask)


def after(value, *others):
    return lax.optimization_barrier((value,) + others)[0]


def local(
    atmos,
    cotangent,
    ocean,
    sea_mask,
    spectral_weight,
    coupling,
    flux_weight,
    conv_weight,
    head_weight,
):
    atmos = atmos.transpose(1, 0, 2)
    cotangent = cotangent.transpose(1, 0, 2)
    ocean = ocean.transpose(1, 0, 2)
    ring = range(8)
    east = [(k, (k + 1) % 8) for k in ring]
    west = [((k + 1) % 8, k) for k in ring]
    swap = [(0, 1), (1, 0)]
    lon_table, lat_table = make_tables(NLAT, NLON, KMODES, LDEG)

    sent, weights, below, above = pack(
        atmos,
        cotangent,
        ocean,
        sea_mask,
        coupling,
        conv_weight.reshape(720, 128),
        head_weight.T,
    )
    weights_other = lax.ppermute(weights, "group", swap)
    top = lax.ppermute(below, "lat", [(k, k + 1) for k in range(7)])
    bottom = lax.ppermute(above, "lat", [(k + 1, k) for k in range(7)])
    sent, weights_other, top, bottom = lax.optimization_barrier(
        (sent, weights_other, top, bottom)
    )
    got = lax.all_to_all(sent, ("lat", "lon"), split_axis=0, concat_axis=0, tiled=True)
    sent_back, grad_spectral = spectral(
        got, arrange_lon(lon_table), arrange_lat(lat_table), spectral_weight
    )
    returned = lax.all_to_all(sent_back, ("lat", "lon"), split_axis=0, concat_axis=0, tiled=True)
    atmos_next, flux, to_east, to_west = unpack_flux(returned, flux_weight, ocean, top, bottom)
    across = [(8 * g + k, 8 * (1 - g) + (k + 1) % 8) for g in range(2) for k in ring]
    counter = [(8 * g + k, 8 * (1 - g) + (k - 1) % 8) for g in range(2) for k in ring]
    fluxes = [
        flux,
        lax.ppermute(flux, "group", swap),
        lax.ppermute(to_east, "lon", east),
        lax.ppermute(flux, ("group", "lon"), across),
        lax.ppermute(to_west, "lon", west),
        lax.ppermute(flux, ("group", "lon"), counter),
    ]
    grad_atmos, taps, conv, head = unpack_taps(
        after(returned, flux), weights, weights_other, ocean, top, bottom
    )
    ocean_next = ocean_step(fluxes, taps, conv, head, ocean, sea_mask)
    return (
        atmos_next.transpose(1, 0, 2),
        grad_atmos.transpose(1, 0, 2),
        grad_spectral,
        ocean_next.transpose(1, 0, 2),
    )


def solution(mesh):
    in_specs = (
        P("group", "lat", "lon"),
        P("group", "lat", "lon"),
        P(None, "lat", "lon"),
        P("lat", "lon"),
        P(("group", "lat", "lon"), None),
        P("group"),
        P(None, "group"),
        P(None, None, None, "group"),
        P("group", None),
    )
    out_specs = (
        P("group", "lat", "lon"),
        P("group", "lat", "lon"),
        P(("group", "lat", "lon"), None),
        P(None, "lat", "lon"),
    )
    return jax.shard_map(local, mesh=mesh, in_specs=in_specs, out_specs=out_specs, check_vma=False)
```

```python
import math

import jax
import jax.numpy as jnp
import ml_dtypes
import numpy as np
from jax import lax
from jax.experimental import pallas as pl
from jax.experimental.pallas import tpu as pltpu
from jax.sharding import PartitionSpec as P

NLAT = 720
NLON = 1024
KMODES = 384
LDEG = 384
ROWS = 90
COLS = 128
CH = 128
OWNERS = 64
SENT = 360
BACK = 368
PITCH = CH + 1
F32 = jnp.float32
BF16 = jnp.bfloat16
MIB = 1024 * 1024
GELU_ONE = math.sqrt(2.0 / math.pi)
GELU_THREE = 0.044715 * GELU_ONE


def make_tables(nlat, nlon, kmodes, ldeg):
    column = np.arange(nlon, dtype=np.int64)[:, None]
    wavenum = np.arange(kmodes, dtype=np.int64)[None, :]
    step = np.float32(2.0 * math.pi / nlon)
    phase_cos = (column * wavenum % nlon).astype(np.float32) * step
    phase_sin = (column * (wavenum + 1) % nlon).astype(np.float32) * step
    lon_table = np.concatenate([np.cos(phase_cos), np.sin(phase_sin)], axis=1)
    lon_table = lon_table * np.float32(math.sqrt(2.0 / nlon))
    latrow = np.arange(nlat, dtype=np.int64)[:, None]
    degree = np.arange(ldeg, dtype=np.int64)[None, :]
    phase_lat = (degree * (2 * latrow + 1) % (4 * nlat)).astype(np.float32) * np.float32(
        math.pi / (2 * nlat)
    )
    lat_table = np.cos(phase_lat) * np.float32(math.sqrt(2.0 / nlat))
    return (lon_table.astype(ml_dtypes.bfloat16), lat_table.astype(ml_dtypes.bfloat16))


def arrange_lon(lon_table):
    cosines = np.arange(KMODES)
    sines = np.arange(1, KMODES + 1)
    place = np.concatenate([cosines, sines])
    zero = lon_table[:256, place % 4 == 0]
    two = lon_table[:256, place % 4 == 2]
    odd = lon_table[:512, place % 2 == 1]
    blank = np.zeros((256, 64), lon_table.dtype)
    return (
        np.concatenate([zero, blank], axis=1),
        np.concatenate([blank, two], axis=1),
        odd,
    )


def arrange_lat(lat_table):
    blocks = lat_table.reshape(4, 2, ROWS, LDEG)
    main = blocks[:, :, :80].reshape(4, 160, LDEG)
    middle = blocks[:, :, 80:88].reshape(4, 16, LDEG)
    last = blocks[:, :, 88:90]
    made = []
    for m in range(4):
        tail = np.zeros((4, 2, 4, 2, LDEG), lat_table.dtype)
        tail[:, :, m] = last
        tail = tail.reshape(4, 16, LDEG)
        made.append(np.concatenate([main, middle, tail], axis=1).reshape(768, LDEG))
    return np.stack(made)


def even(axis):
    return lax.rem(lax.axis_index(axis), 2) == 0


def pack_kernel(
    atmos,
    cotangent,
    ocean,
    mask,
    coupling,
    out,
    border_one,
    border_two,
    in_a,
    in_c,
    warm,
    sea_cells,
    gains,
    held_a,
    held_c,
    last,
    sems,
):
    def fetches(i, rows):
        span = pl.ds(16 * i, rows)
        return [
            pltpu.make_async_copy(atmos.at[span], in_a.at[span], sems.at[0, i]),
            pltpu.make_async_copy(cotangent.at[span], in_c.at[span], sems.at[1, i]),
        ]

    surface = [
        pltpu.make_async_copy(ocean.at[:, pl.ds(0, 16), :], warm, sems.at[2, 0]),
        pltpu.make_async_copy(mask, sea_cells, sems.at[2, 1]),
        pltpu.make_async_copy(coupling, gains, sems.at[2, 2]),
    ]
    facing = jnp.where(even("lat"), ROWS - 1, 0)
    others = [
        pltpu.make_async_copy(ocean.at[pl.ds(facing, 1)], border_one, sems.at[2, 5]),
        pltpu.make_async_copy(ocean.at[pl.ds(ROWS - 1 - facing, 1)], border_two, sems.at[3, 0]),
    ]
    for copy in surface:
        copy.start()
    for i in range(6):
        for copy in fetches(i, 16 if i < 5 else 10):
            copy.start()
    for copy in others:
        copy.start()
    for copy in surface:
        copy.wait()
    gain = jnp.broadcast_to(gains[...], (CH, COLS)).T

    def widen(i, rows):
        for copy in fetches(i, rows):
            copy.wait()
        for r in range(rows):
            row = 16 * i + r
            sea = sea_cells[pl.ds(row, 1), :].astype(F32)
            forcing = sea * warm[row].astype(F32)[0:1]
            held_a[r * PITCH : r * PITCH + CH, :] = in_a[row].astype(F32) + forcing * gain
            held_c[r * PITCH : r * PITCH + CH, :] = in_c[row].astype(F32)

    @pl.loop(0, 5)
    def _(i):
        widen(i, 16)
        base = pl.multiple_of(64 * i, 64)
        for ch in range(CH):
            for f, held in enumerate((held_a, held_c)):
                at = base + 32 * f + 16 * (ch % 2)
                out[ch // 2, pl.ds(at, 16), :] = held[pl.ds(ch, 16, stride=PITCH), :].astype(BF16)

    widen(5, 10)
    for d in range(OWNERS):
        for f, held in enumerate((held_a, held_c)):
            pair = [held[pl.ds(2 * d + c, 8, stride=PITCH), :] for c in range(2)]
            out[d, 320 + 16 * f : 336 + 16 * f, :] = jnp.concatenate(pair, axis=0).astype(BF16)
            for t in range(2):
                both = held[(8 + t) * PITCH + 2 * d : (8 + t) * PITCH + 2 * d + 2, :]
                for c in range(2):
                    row = 4 * f + 2 * c + t
                    last[d, row : row + 1, :] = both[c : c + 1]
        out[d, 352:360, :] = last[d].astype(BF16)

    for copy in others:
        copy.wait()


def vmem():
    return pl.BlockSpec(memory_space=pltpu.VMEM)


def near(array):
    return pltpu.with_memory_space_constraint(array, pltpu.VMEM)


def in_hbm():
    return pl.BlockSpec(memory_space=pltpu.HBM)


def pack(atmos, cotangent, ocean, sea_mask, coupling):
    given = (atmos, cotangent, ocean, sea_mask, coupling[None, :])
    return pl.pallas_call(
        pack_kernel,
        in_specs=[in_hbm()] * 5,
        out_specs=[vmem()] * 3,
        out_shape=[
            pltpu.VMEM((OWNERS, SENT, COLS), BF16),
            pltpu.VMEM((1, 76, COLS), BF16),
            pltpu.VMEM((1, 76, COLS), BF16),
        ],
        scratch_shapes=[
            pltpu.VMEM((ROWS, CH, COLS), BF16),
            pltpu.VMEM((ROWS, CH, COLS), BF16),
            pltpu.VMEM((ROWS, 16, COLS), BF16),
            pltpu.VMEM((ROWS, COLS), jnp.int32),
            pltpu.VMEM((1, CH), F32),
            pltpu.VMEM((16 * PITCH, COLS), F32),
            pltpu.VMEM((16 * PITCH, COLS), F32),
            pltpu.VMEM((OWNERS, 8, COLS), F32),
            pltpu.SemaphoreType.DMA((4, 6)),
        ],
        compiler_params=pltpu.CompilerParams(vmem_limit_bytes=14 * MIB),
        name="pack",
    )(*[pltpu.with_memory_space_constraint(array, pltpu.HBM) for array in given])


def spectral_kernel(
    got,
    lon_zero,
    lon_two,
    lon_odd,
    back_zero,
    back_two,
    back_odd,
    lat,
    lat_back,
    weight,
    out,
    grad,
    coef,
    kept,
    back,
    edge_in,
    edge,
    halo,
):
    edge_in[...] = jnp.zeros_like(edge_in)
    edge[...] = jnp.zeros_like(edge)

    def dot(one, two):
        return jnp.dot(one, two, preferred_element_type=F32)

    @pl.loop(0, 4)
    def _(p):
        found = []
        for a in range(2):
            first = 16 * p + 8 * a
            quarter = [
                jnp.concatenate([got[first + 2 * q + h].astype(F32) for h in range(2)], axis=1)
                for q in range(4)
            ]
            even_0 = quarter[0] + quarter[2]
            even_1 = quarter[1] + quarter[3]
            odd = jnp.concatenate(
                [(quarter[0] - quarter[2]).astype(BF16), (quarter[1] - quarter[3]).astype(BF16)],
                axis=1,
            )
            zero = dot((even_0 + even_1).astype(BF16), lon_zero[...])
            two = dot((even_0 - even_1).astype(BF16), lon_two[...])
            found.append(
                [
                    zero[:, 0:128],
                    zero[:, 128:256] + two[:, 0:128],
                    two[:, 128:256],
                    dot(odd, lon_odd[...]),
                ]
            )
        for n, cols in enumerate(
            (slice(0, 128), slice(128, 256), slice(256, 384), slice(384, 768))
        ):
            for m in range(4):
                for a in range(2):
                    for i in range(5):
                        coef[m, p, 80 * a + 16 * i : 80 * a + 16 * i + 16, cols] = found[a][n][
                            64 * i + 16 * m : 64 * i + 16 * m + 16
                        ].astype(BF16)
                coef[m, p, 160:176, cols] = jnp.concatenate(
                    [found[a][n][320 + 8 * m : 328 + 8 * m] for a in range(2)], axis=0
                ).astype(BF16)
                coef[m, p, 176:192, cols] = jnp.concatenate(
                    [found[a][n][352:360] for a in range(2)], axis=0
                ).astype(BF16)
        for a in range(2):
            block = 2 * p + a
            for o in range(8):
                lanes = slice(128 * o, 128 * o + 128)
                low = got[8 * block + o, 352:360, :].astype(F32)
                for c in range(2):
                    high = got[8 * block + o, 16 * c : 16 * c + 16, :].astype(F32)
                    edge_in[block + 2, c : c + 1, lanes] = low[2 * c + 1 : 2 * c + 2]
                    edge_in[block, 2 + c : 3 + c, lanes] = high[0:1]

    for c in range(2):
        scale = jnp.broadcast_to(weight[c : c + 1, :], (256, LDEG)).T
        total = jnp.zeros((LDEG, 128), F32)
        for n in range(3):
            cols = slice(256 * n, 256 * n + 256)
            spectra = []
            for f in range(2):
                m = 2 * f + c
                found = dot(lat[m], coef[m, :, :, cols].reshape(768, 256))
                kept[m, :, cols] = (found * scale).astype(BF16)
                spectra.append(found)
            product = spectra[0] * spectra[1]
            total = total + product[:, :128] + product[:, 128:]
        grad[c : c + 1, :] = jnp.sum(total.T, axis=0, keepdims=True) / KMODES
    for n in range(3):
        cols = slice(256 * n, 256 * n + 256)
        tails = [jnp.zeros((16, 256), F32) for _ in range(4)]
        for m in range(4):
            found = dot(lat_back[m], kept[m, :, cols])
            for p in range(4):
                base = 192 * p
                back[p, 160 * m : 160 * m + 160, cols] = found[base : base + 160].astype(BF16)
                back[p, 640 + 16 * m : 656 + 16 * m, cols] = found[
                    base + 160 : base + 176
                ].astype(BF16)
                tail = found[base + 176 : base + 192]
                tails[p] = tails[p] + tail
                if m < 2:
                    for a in range(2):
                        block = 2 * p + a
                        row = 8 * a + 2 * m + 1
                        edge[block + 2, m : m + 1, cols] = tail[row : row + 1]
                        edge[block, 2 + m : 3 + m, cols] = found[base + 80 * a : base + 80 * a + 1]
        for p in range(4):
            back[p, 704:720, cols] = tails[p].astype(BF16)

    def inverse(rows):
        zero = dot(rows[:, 0:256], back_zero[...])
        two = dot(rows[:, 128:384], back_two[...])
        for n in range(2):
            even = zero + two if n == 0 else zero - two
            odd = dot(rows[:, 384:768], back_odd[:, 256 * n : 256 * n + 256])
            yield 2 * n, even + odd
            yield 2 * n + 4, even - odd

    for o, found in inverse(edge[1:9].reshape(64, 768).astype(BF16)):
        lanes = slice(128 * o, 128 * o + 256)
        halo[:, :, lanes] = found.reshape(8, 8, 256) + edge_in[1:9, :, lanes]

    @pl.loop(0, 4)
    def _(p):
        for first, found in inverse(back[p]):
            for half in range(2):
                o = first + half
                lanes = slice(128 * half, 128 * half + 128)
                for a in range(2):
                    d = 16 * p + 8 * a + o
                    for i in range(5):
                        for m in range(4):
                            at = 160 * m + 80 * a + 16 * i
                            to = 64 * i + 16 * m
                            out[d, to : to + 16, :] = (
                                found[at : at + 16, lanes] + got[d, to : to + 16, :].astype(F32)
                            ).astype(BF16)
                    for f in range(2):
                        at = 640 + 32 * f + 8 * a
                        to = 320 + 16 * f
                        pair = jnp.concatenate(
                            [found[at : at + 8, lanes], found[at + 16 : at + 24, lanes]], axis=0
                        )
                        out[d, to : to + 16, :] = (
                            pair + got[d, to : to + 16, :].astype(F32)
                        ).astype(BF16)
                    at = 704 + 8 * a
                    low = found[at : at + 8, lanes] + got[d, 352:360, :].astype(F32)
                    beyond = halo[2 * p + a, :, 128 * o : 128 * o + 128]
                    out[d, 352:368, :] = jnp.concatenate([low, beyond], axis=0).astype(BF16)


def spectral(got, lon, lat, weight):
    tables = list(lon) + [table.T for table in lon] + [lat.transpose(0, 2, 1), lat]
    return pl.pallas_call(
        spectral_kernel,
        in_specs=[vmem()] * 10,
        out_specs=[vmem(), vmem()],
        out_shape=[
            pltpu.VMEM((OWNERS, BACK, COLS), BF16),
            jax.ShapeDtypeStruct((2, LDEG), F32),
        ],
        scratch_shapes=[
            pltpu.VMEM((4, 4, 192, 768), BF16),
            pltpu.VMEM((4, LDEG, 768), BF16),
            pltpu.VMEM((4, 720, 768), BF16),
            pltpu.VMEM((10, 8, NLON), F32),
            pltpu.VMEM((10, 8, 768), F32),
            pltpu.VMEM((8, 8, NLON), F32),
        ],
        compiler_params=pltpu.CompilerParams(vmem_limit_bytes=20 * MIB),
        name="spectral",
    )(near(got), *[near(jnp.asarray(np.ascontiguousarray(table))) for table in tables], weight)


def spread(sent_back, i, field, held):
    base = pl.multiple_of(64 * i, 64) + 32 * field
    for ch in range(CH):
        at = base + 16 * (ch % 2)
        held[pl.ds(ch, 16, stride=PITCH), :] = sent_back[ch // 2, pl.ds(at, 16), :].astype(F32)


def spread_last(sent_back, field, held):
    for d in range(OWNERS):
        near = sent_back[d, 320 + 16 * field : 336 + 16 * field, :].astype(F32)
        last = sent_back[d, 352:368, :].astype(F32)
        for c in range(2):
            held[pl.ds(2 * d + c, 8, stride=PITCH), :] = near[8 * c : 8 * c + 8]
            for t in range(2):
                row = 4 * field + 2 * c + t
                at = (8 + t) * PITCH + 2 * d + c
                held[at : at + 1, :] = last[row : row + 1]


def unpack_rows(sent_back, field, out, held, staged, sems, visit):
    def send(i, rows):
        span = pl.ds(16 * i, rows)
        return pltpu.make_async_copy(staged.at[span], out.at[span], sems.at[i])

    @pl.loop(0, 5)
    def _(i):
        spread(sent_back, i, field, held)
        for r in range(16):
            staged[16 * i + r] = held[r * PITCH : r * PITCH + CH, :].astype(BF16)
            visit(16 * i + r)
        send(i, 16).start()

    spread_last(sent_back, field, held)
    for r in range(10):
        staged[80 + r] = held[r * PITCH : r * PITCH + CH, :].astype(BF16)
        visit(80 + r)
    send(5, 10).start()

    def finish():
        for i in range(6):
            send(i, 16 if i < 5 else 10).wait()

    return finish


def outside_rows(got_one, got_two):
    one, two = got_one[0], got_two[0]
    return jnp.where(even("lat"), two, one), jnp.where(even("lat"), one, two)


def unpack_flux_kernel(
    sent_back,
    weight,
    ocean,
    got_one,
    got_two,
    head,
    out,
    flux,
    to_group,
    to_near,
    to_far,
    held,
    staged,
    outside,
    found,
    sems,
):
    def put(row, cells):
        sums = jnp.dot(weight[...], cells, preferred_element_type=F32)
        found[pl.ds(4 * row, 4), :] = sums[0:4]

    finish = unpack_rows(
        sent_back, 0, out, held, staged, sems, lambda row: put(row + 1, staged[row])
    )
    for d in range(OWNERS):
        beyond = sent_back[d, 352:368, :].astype(F32)
        for side in range(2):
            outside[side, 2 * d : 2 * d + 2, :] = beyond[8 + 2 * side : 10 + 2 * side]
    put(0, outside[0].astype(BF16))
    put(91, outside[1].astype(BF16))

    lane = lax.broadcasted_iota(jnp.int32, (76, COLS), 1)

    def gather(row, cells, kept):
        at = lane == row
        return (
            jnp.where(at, pltpu.roll(cells, lax.rem(row + 1, COLS), 1), kept[0]),
            jnp.where(at, pltpu.roll(cells, row, 1), kept[1]),
        )

    blank = jnp.zeros((76, COLS), BF16)
    top, bottom = outside_rows(got_one, got_two)
    edges = gather(jnp.int32(0), top, (blank, blank))
    edges = gather(jnp.int32(91), bottom, edges)
    edges = lax.fori_loop(
        0, ROWS, lambda row, kept: gather(row + 1, ocean[row], kept), edges, unroll=18
    )

    sums = found[...].astype(BF16)
    flux[...] = sums
    near_edge = jnp.where(even("lon"), edges[0], edges[1])
    far_edge = jnp.where(even("lon"), edges[1], edges[0])
    for message, rows in ((to_near, near_edge), (to_far, far_edge), (to_group, head[...])):
        message[0:368, :] = sums
        message[368:448, :] = jnp.concatenate(
            [rows.astype(F32), jnp.zeros((4, COLS), F32)], axis=0
        ).astype(BF16)
    finish()


def unpack_taps_kernel(
    sent_back,
    weights,
    weights_other,
    ocean,
    got_one,
    got_two,
    out,
    taps,
    conv,
    held,
    staged,
    sems,
):
    finish = unpack_rows(sent_back, 1, out, held, staged, sems, lambda row: None)

    for half, given in enumerate((weights, weights_other)):
        rows = slice(128 * half, 128 * half + 128)
        wide = jnp.concatenate([given[...].astype(F32), jnp.zeros((48, 128), F32)], axis=0)
        conv[rows, :] = wide.T.astype(BF16)

    def build(row, cells):
        wide = jnp.concatenate([cells, jnp.zeros((4, COLS), BF16)], axis=0)
        base = pl.multiple_of(240 * row, 16)
        taps[pl.ds(base, 80), :] = pltpu.roll(wide, 1, 1)
        taps[pl.ds(base + 80, 80), :] = wide
        taps[pl.ds(base + 160, 80), :] = pltpu.roll(wide, COLS - 1, 1)

    top, bottom = outside_rows(got_one, got_two)
    build(0, top)
    build(91, bottom)
    taps[92 * 240 :, :] = jnp.zeros((48, COLS), BF16)

    @pl.loop(0, ROWS, unroll=18)
    def _(row):
        build(row + 1, ocean[row])

    finish()


def unpack_scratch():
    return [pltpu.VMEM((16 * PITCH, COLS), F32), pltpu.VMEM((ROWS, CH, COLS), BF16)]


def unpack_flux(sent_back, weight, ocean, top, bottom, head):
    return pl.pallas_call(
        unpack_flux_kernel,
        in_specs=[vmem()] * 6,
        out_specs=[in_hbm(), vmem(), vmem(), vmem(), vmem()],
        out_shape=[
            jax.ShapeDtypeStruct((ROWS, CH, COLS), BF16),
            jax.ShapeDtypeStruct((368, COLS), BF16),
            jax.ShapeDtypeStruct((448, COLS), BF16),
            jax.ShapeDtypeStruct((448, COLS), BF16),
            jax.ShapeDtypeStruct((448, COLS), BF16),
        ],
        scratch_shapes=unpack_scratch()
        + [
            pltpu.VMEM((2, CH, COLS), F32),
            pltpu.VMEM((368, COLS), F32),
            pltpu.SemaphoreType.DMA((6,)),
        ],
        compiler_params=pltpu.CompilerParams(vmem_limit_bytes=12 * MIB),
        name="unpack_flux",
    )(near(sent_back), weight, near(ocean), top, bottom, head)


def unpack_taps(sent_back, weights, weights_other, ocean, top, bottom):
    return pl.pallas_call(
        unpack_taps_kernel,
        in_specs=[vmem()] * 6,
        out_specs=[in_hbm(), vmem(), vmem()],
        out_shape=[
            jax.ShapeDtypeStruct((ROWS, CH, COLS), BF16),
            pltpu.VMEM((92 * 240 + 48, COLS), BF16),
            pltpu.VMEM((256, 768), BF16),
        ],
        scratch_shapes=unpack_scratch() + [pltpu.SemaphoreType.DMA((6,))],
        compiler_params=pltpu.CompilerParams(vmem_limit_bytes=12 * MIB),
        cost_estimate=pl.CostEstimate(flops=0, bytes_accessed=12_000_000, transcendentals=0),
        name="unpack_taps",
    )(near(sent_back), weights, weights_other, near(ocean), top, bottom)


def ocean_kernel(
    own,
    other,
    near_one,
    near_other,
    far_one,
    far_other,
    unfinished,
    conv,
    ocean,
    mask,
    out,
    taps,
    head,
    fluxes,
    hidden,
    staged,
    sems,
):
    def whole(one, two):
        total = one[0:368, :].astype(F32) + two[0:368, :].astype(F32)
        return total.astype(BF16).astype(F32)

    column = lax.broadcasted_iota(jnp.int32, (368, COLS), 1)
    def sides(one, two):
        return jnp.where(even("lon"), two, one), jnp.where(even("lon"), one, two)

    middle = whole(own, other)
    west, east = sides(whole(near_one, near_other), whole(far_one, far_other))
    west = pltpu.roll(west, 1, 1)
    east = pltpu.roll(east, COLS - 1, 1)
    fluxes[0] = jnp.where(column == 0, west, pltpu.roll(middle, 1, 1))
    fluxes[1] = middle
    fluxes[2] = jnp.where(column == COLS - 1, east, pltpu.roll(middle, COLS - 1, 1))

    head[:, 0:128] = own[368:448, :]
    head[:, 128:256] = other[368:448, :]

    lane = lax.broadcasted_iota(jnp.int32, (80, COLS), 1)
    first_edge, final_edge = sides(near_one[368:448, :], far_one[368:448, :])

    taps[92 * 240 :, :] = jnp.zeros((48, COLS), BF16)

    def complete(row):
        base = pl.multiple_of(240 * row, 16)
        first = pltpu.roll(first_edge, lax.rem(COLS - row, COLS), 1)
        final = pltpu.roll(final_edge, COLS - 1 - row, 1)
        shifts = (
            jnp.where(lane == 0, first, unfinished[pl.ds(base, 80), :]),
            unfinished[pl.ds(base + 80, 80), :],
            jnp.where(lane == COLS - 1, final, unfinished[pl.ds(base + 160, 80), :]),
        )
        for b, cells in enumerate(shifts):
            at = base + 80 * b
            taps[pl.ds(at, 64), :] = cells[0:64]
            rest = [cells[64:80].astype(F32)[0:12], fluxes[b, pl.ds(4 * row, 4), :]]
            taps[pl.ds(at + 64, 16), :] = jnp.concatenate(rest, axis=0).astype(BF16)

    def send(g):
        span = pl.ds(10 * g, 10)
        return pltpu.make_async_copy(staged.at[span], out.at[span], sems.at[g])

    def window(row):
        return taps[pl.ds(pl.multiple_of(240 * row, 16), 768), :]

    def convolve(g, more):
        for pair in range(5):
            first = 10 * g + 2 * pair
            around = jnp.concatenate([window(first), window(first + 1)], axis=1)
            x = jnp.dot(conv[...], around, preferred_element_type=F32)
            bent = jnp.tanh(x * (GELU_ONE + GELU_THREE * (x * x)))
            half = 0.5 * x
            hidden[lax.rem(g, 2), :, 256 * pair : 256 * pair + 256] = (half + half * bent).astype(
                BF16
            )
            if more:
                for k in range(2):
                    complete(first + 12 + k)

    def decode(g):
        delta = jnp.dot(head[...], hidden[lax.rem(g, 2)], preferred_element_type=F32)
        for k in range(10):
            row = 10 * g + k
            sea = mask[pl.ds(row, 1), :].astype(F32)
            staged[row] = (
                ocean[row].astype(F32) + sea * delta[0:76, COLS * k : COLS * k + COLS]
            ).astype(BF16)
        send(g).start()

    for row in range(12):
        complete(jnp.int32(row))
    convolve(jnp.int32(0), True)

    @pl.loop(1, 8)
    def _(g):
        convolve(g, True)
        decode(g - 1)

    convolve(jnp.int32(8), False)
    decode(jnp.int32(7))
    decode(jnp.int32(8))
    for g in range(9):
        send(g).wait()


def ocean_step(fluxes, taps, conv, ocean, sea_mask):
    return pl.pallas_call(
        ocean_kernel,
        in_specs=[vmem()] * 10,
        out_specs=in_hbm(),
        out_shape=jax.ShapeDtypeStruct((ROWS, 76, COLS), BF16),
        scratch_shapes=[
            pltpu.VMEM((92 * 240 + 48, COLS), BF16),
            pltpu.VMEM((80, 256), BF16),
            pltpu.VMEM((3, 368, COLS), F32),
            pltpu.VMEM((2, 256, 1280), BF16),
            pltpu.VMEM((ROWS, 76, COLS), BF16),
            pltpu.SemaphoreType.DMA((9,)),
        ],
        compiler_params=pltpu.CompilerParams(vmem_limit_bytes=14 * MIB),
        name="ocean",
    )(*fluxes, near(taps), near(conv), near(ocean), sea_mask)


def after(value, *others):
    return lax.optimization_barrier((value,) + others)[0]


def local(
    atmos,
    cotangent,
    ocean,
    sea_mask,
    spectral_weight,
    coupling,
    flux_weight,
    conv_weight,
    head_weight,
):
    atmos = atmos.transpose(1, 0, 2)
    cotangent = cotangent.transpose(1, 0, 2)
    ocean = ocean.transpose(1, 0, 2)
    near_pairs = [(k, k ^ 1) for k in range(8)]
    far_pairs = [(k, (k + 1 - 2 * (k % 2 == 0)) % 8) for k in range(8)]
    swap = [(0, 1), (1, 0)]
    lon_table, lat_table = make_tables(NLAT, NLON, KMODES, LDEG)

    barrier = lax.optimization_barrier
    sent, border_one, border_two = pack(atmos, cotangent, ocean, sea_mask, coupling)
    got = lax.all_to_all(sent, ("lat", "lon"), split_axis=0, concat_axis=0, tiled=True)

    conv = conv_weight.reshape(720, 128)
    got, conv, border_one, border_two = barrier((got, conv, border_one, border_two))
    conv_other = lax.ppermute(conv, "group", swap)
    got_one = lax.ppermute(border_one, "lat", near_pairs)
    got_two = lax.ppermute(border_two, "lat", [pair for pair in far_pairs if set(pair) != {0, 7}])
    sent_back, grad_spectral = spectral(
        got, arrange_lon(lon_table), arrange_lat(lat_table), spectral_weight
    )
    sent_back, conv_other, got_one, got_two = barrier(
        (sent_back, conv_other, got_one, got_two)
    )
    returned = lax.all_to_all(sent_back, ("lat", "lon"), split_axis=0, concat_axis=0, tiled=True)
    atmos_next, flux, to_group, to_near, to_far = unpack_flux(
        returned, flux_weight, ocean, got_one, got_two, head_weight.T
    )

    def crossed(pairs):
        return [(8 * g + k, 8 * (1 - g) + to) for g in range(2) for k, to in pairs]

    fluxes = [
        to_group,
        lax.ppermute(to_group, "group", swap),
        lax.ppermute(to_near, "lon", near_pairs),
        lax.ppermute(flux, ("group", "lon"), crossed(near_pairs)),
        lax.ppermute(to_far, "lon", far_pairs),
        lax.ppermute(flux, ("group", "lon"), crossed(far_pairs)),
    ]
    grad_atmos, taps, conv = unpack_taps(
        after(returned, flux), conv, conv_other, ocean, got_one, got_two
    )
    ocean_next = ocean_step(fluxes, taps, conv, ocean, sea_mask)
    return (
        atmos_next.transpose(1, 0, 2),
        grad_atmos.transpose(1, 0, 2),
        grad_spectral,
        ocean_next.transpose(1, 0, 2),
    )


def solution(mesh):
    in_specs = (
        P("group", "lat", "lon"),
        P("group", "lat", "lon"),
        P(None, "lat", "lon"),
        P("lat", "lon"),
        P(("group", "lat", "lon"), None),
        P("group"),
        P(None, "group"),
        P(None, None, None, "group"),
        P("group", None),
    )
    out_specs = (
        P("group", "lat", "lon"),
        P("group", "lat", "lon"),
        P(("group", "lat", "lon"), None),
        P(None, "lat", "lon"),
    )
    return jax.shard_map(local, mesh=mesh, in_specs=in_specs, out_specs=out_specs, check_vma=False)
```

```python
import math

import jax
import jax.numpy as jnp
import ml_dtypes
import numpy as np
from jax import lax
from jax.experimental import pallas as pl
from jax.experimental.pallas import tpu as pltpu
from jax.sharding import PartitionSpec as P

NLAT = 720
NLON = 1024
KMODES = 384
LDEG = 384
ROWS = 90
COLS = 128
CH = 128
OWNERS = 64
SENT = 360
BACK = 368
PITCH = CH + 1
F32 = jnp.float32
BF16 = jnp.bfloat16
MIB = 1024 * 1024
GELU_ONE = math.sqrt(2.0 / math.pi)
GELU_THREE = 0.044715 * GELU_ONE


def make_tables(nlat, nlon, kmodes, ldeg):
    column = np.arange(nlon, dtype=np.int64)[:, None]
    wavenum = np.arange(kmodes, dtype=np.int64)[None, :]
    step = np.float32(2.0 * math.pi / nlon)
    phase_cos = (column * wavenum % nlon).astype(np.float32) * step
    phase_sin = (column * (wavenum + 1) % nlon).astype(np.float32) * step
    lon_table = np.concatenate([np.cos(phase_cos), np.sin(phase_sin)], axis=1)
    lon_table = lon_table * np.float32(math.sqrt(2.0 / nlon))
    latrow = np.arange(nlat, dtype=np.int64)[:, None]
    degree = np.arange(ldeg, dtype=np.int64)[None, :]
    phase_lat = (degree * (2 * latrow + 1) % (4 * nlat)).astype(np.float32) * np.float32(
        math.pi / (2 * nlat)
    )
    lat_table = np.cos(phase_lat) * np.float32(math.sqrt(2.0 / nlat))
    return (lon_table.astype(ml_dtypes.bfloat16), lat_table.astype(ml_dtypes.bfloat16))


def arrange_lon(lon_table):
    cosines = np.arange(KMODES)
    sines = np.arange(1, KMODES + 1)
    place = np.concatenate([cosines, sines])
    zero = lon_table[:256, place % 4 == 0]
    two = lon_table[:256, place % 4 == 2]
    odd = lon_table[:512, place % 2 == 1]
    blank = np.zeros((256, 64), lon_table.dtype)
    return (
        np.concatenate([zero, blank], axis=1),
        np.concatenate([blank, two], axis=1),
        odd,
    )


def arrange_lat(lat_table):
    blocks = lat_table.reshape(4, 2, ROWS, LDEG)
    main = blocks[:, :, :80].reshape(4, 160, LDEG)
    middle = blocks[:, :, 80:88].reshape(4, 16, LDEG)
    last = blocks[:, :, 88:90]
    made = []
    for m in range(4):
        tail = np.zeros((4, 2, 4, 2, LDEG), lat_table.dtype)
        tail[:, :, m] = last
        tail = tail.reshape(4, 16, LDEG)
        made.append(np.concatenate([main, middle, tail], axis=1).reshape(768, LDEG))
    return np.stack(made)


def even(axis):
    return lax.rem(lax.axis_index(axis), 2) == 0


def pack_kernel(
    atmos,
    cotangent,
    ocean,
    mask,
    coupling,
    out,
    border_one,
    border_two,
    in_a,
    in_c,
    warm,
    sea_cells,
    gains,
    held_a,
    held_c,
    last,
    sems,
):
    def fetches(i, rows):
        span = pl.ds(16 * i, rows)
        return [
            pltpu.make_async_copy(atmos.at[span], in_a.at[span], sems.at[0, i]),
            pltpu.make_async_copy(cotangent.at[span], in_c.at[span], sems.at[1, i]),
        ]

    surface = [
        pltpu.make_async_copy(ocean.at[:, pl.ds(0, 16), :], warm, sems.at[2, 0]),
        pltpu.make_async_copy(mask, sea_cells, sems.at[2, 1]),
        pltpu.make_async_copy(coupling, gains, sems.at[2, 2]),
    ]
    facing = jnp.where(even("lat"), ROWS - 1, 0)
    others = [
        pltpu.make_async_copy(ocean.at[pl.ds(facing, 1)], border_one, sems.at[2, 5]),
        pltpu.make_async_copy(ocean.at[pl.ds(ROWS - 1 - facing, 1)], border_two, sems.at[3, 0]),
    ]
    for copy in surface:
        copy.start()
    for i in range(6):
        for copy in fetches(i, 16 if i < 5 else 10):
            copy.start()
    for copy in others:
        copy.start()
    for copy in surface:
        copy.wait()
    gain = jnp.broadcast_to(gains[...], (CH, COLS)).T

    def widen(i, rows):
        for copy in fetches(i, rows):
            copy.wait()
        for r in range(rows):
            row = 16 * i + r
            sea = sea_cells[pl.ds(row, 1), :].astype(F32)
            forcing = sea * warm[row].astype(F32)[0:1]
            held_a[r * PITCH : r * PITCH + CH, :] = in_a[row].astype(F32) + forcing * gain
            held_c[r * PITCH : r * PITCH + CH, :] = in_c[row].astype(F32)

    @pl.loop(0, 5)
    def _(i):
        widen(i, 16)
        base = pl.multiple_of(64 * i, 64)
        for ch in range(CH):
            for f, held in enumerate((held_a, held_c)):
                at = base + 32 * f + 16 * (ch % 2)
                out[ch // 2, pl.ds(at, 16), :] = held[pl.ds(ch, 16, stride=PITCH), :].astype(BF16)

    widen(5, 10)
    for d in range(OWNERS):
        for f, held in enumerate((held_a, held_c)):
            pair = [held[pl.ds(2 * d + c, 8, stride=PITCH), :] for c in range(2)]
            out[d, 320 + 16 * f : 336 + 16 * f, :] = jnp.concatenate(pair, axis=0).astype(BF16)
            for t in range(2):
                both = held[(8 + t) * PITCH + 2 * d : (8 + t) * PITCH + 2 * d + 2, :]
                for c in range(2):
                    row = 4 * f + 2 * c + t
                    last[d, row : row + 1, :] = both[c : c + 1]
        out[d, 352:360, :] = last[d].astype(BF16)

    for copy in others:
        copy.wait()


def vmem():
    return pl.BlockSpec(memory_space=pltpu.VMEM)


def near(array):
    return pltpu.with_memory_space_constraint(array, pltpu.VMEM)


def in_hbm():
    return pl.BlockSpec(memory_space=pltpu.HBM)


def pack(atmos, cotangent, ocean, sea_mask, coupling):
    given = (atmos, cotangent, ocean, sea_mask, coupling[None, :])
    return pl.pallas_call(
        pack_kernel,
        in_specs=[in_hbm()] * 5,
        out_specs=[vmem()] * 3,
        out_shape=[
            pltpu.VMEM((OWNERS, SENT, COLS), BF16),
            pltpu.VMEM((1, 76, COLS), BF16),
            pltpu.VMEM((1, 76, COLS), BF16),
        ],
        scratch_shapes=[
            pltpu.VMEM((ROWS, CH, COLS), BF16),
            pltpu.VMEM((ROWS, CH, COLS), BF16),
            pltpu.VMEM((ROWS, 16, COLS), BF16),
            pltpu.VMEM((ROWS, COLS), jnp.int32),
            pltpu.VMEM((1, CH), F32),
            pltpu.VMEM((16 * PITCH, COLS), F32),
            pltpu.VMEM((16 * PITCH, COLS), F32),
            pltpu.VMEM((OWNERS, 8, COLS), F32),
            pltpu.SemaphoreType.DMA((4, 6)),
        ],
        compiler_params=pltpu.CompilerParams(vmem_limit_bytes=14 * MIB),
        name="pack",
    )(*[pltpu.with_memory_space_constraint(array, pltpu.HBM) for array in given])


def spectral_kernel(
    got,
    lon_zero,
    lon_two,
    lon_odd,
    back_zero,
    back_two,
    back_odd,
    lat,
    lat_back,
    weight,
    out,
    grad,
    coef,
    kept,
    back,
    edge_in,
    edge,
    halo,
):
    edge_in[...] = jnp.zeros_like(edge_in)
    edge[...] = jnp.zeros_like(edge)

    def dot(one, two):
        return jnp.dot(one, two, preferred_element_type=F32)

    @pl.loop(0, 4, unroll=4)
    def _(p):
        found = []
        for a in range(2):
            first = 16 * p + 8 * a
            quarter = [
                jnp.concatenate([got[first + 2 * q + h].astype(F32) for h in range(2)], axis=1)
                for q in range(4)
            ]
            even_0 = quarter[0] + quarter[2]
            even_1 = quarter[1] + quarter[3]
            odd = jnp.concatenate(
                [(quarter[0] - quarter[2]).astype(BF16), (quarter[1] - quarter[3]).astype(BF16)],
                axis=1,
            )
            zero = dot((even_0 + even_1).astype(BF16), lon_zero[...])
            two = dot((even_0 - even_1).astype(BF16), lon_two[...])
            found.append(
                [
                    zero[:, 0:128],
                    zero[:, 128:256] + two[:, 0:128],
                    two[:, 128:256],
                    dot(odd, lon_odd[...]),
                ]
            )
        for n, cols in enumerate(
            (slice(0, 128), slice(128, 256), slice(256, 384), slice(384, 768))
        ):
            for m in range(4):
                for a in range(2):
                    for i in range(5):
                        coef[m, p, 80 * a + 16 * i : 80 * a + 16 * i + 16, cols] = found[a][n][
                            64 * i + 16 * m : 64 * i + 16 * m + 16
                        ].astype(BF16)
                coef[m, p, 160:176, cols] = jnp.concatenate(
                    [found[a][n][320 + 8 * m : 328 + 8 * m] for a in range(2)], axis=0
                ).astype(BF16)
                coef[m, p, 176:192, cols] = jnp.concatenate(
                    [found[a][n][352:360] for a in range(2)], axis=0
                ).astype(BF16)
        for a in range(2):
            block = 2 * p + a
            for o in range(8):
                lanes = slice(128 * o, 128 * o + 128)
                low = got[8 * block + o, 352:360, :].astype(F32)
                for c in range(2):
                    high = got[8 * block + o, 16 * c : 16 * c + 16, :].astype(F32)
                    edge_in[block + 2, c : c + 1, lanes] = low[2 * c + 1 : 2 * c + 2]
                    edge_in[block, 2 + c : 3 + c, lanes] = high[0:1]

    for c in range(2):
        scale = jnp.broadcast_to(weight[c : c + 1, :], (256, LDEG)).T
        total = jnp.zeros((LDEG, 128), F32)
        for n in range(3):
            cols = slice(256 * n, 256 * n + 256)
            spectra = []
            for f in range(2):
                m = 2 * f + c
                found = dot(lat[m], coef[m, :, :, cols].reshape(768, 256))
                kept[m, :, cols] = (found * scale).astype(BF16)
                spectra.append(found)
            product = spectra[0] * spectra[1]
            total = total + product[:, :128] + product[:, 128:]
        grad[c : c + 1, :] = jnp.sum(total.T, axis=0, keepdims=True) / KMODES
    for n in range(3):
        cols = slice(256 * n, 256 * n + 256)
        tails = [jnp.zeros((16, 256), F32) for _ in range(4)]
        for m in range(4):
            found = dot(lat_back[m], kept[m, :, cols])
            for p in range(4):
                base = 192 * p
                back[p, 160 * m : 160 * m + 160, cols] = found[base : base + 160].astype(BF16)
                back[p, 640 + 16 * m : 656 + 16 * m, cols] = found[
                    base + 160 : base + 176
                ].astype(BF16)
                tail = found[base + 176 : base + 192]
                tails[p] = tails[p] + tail
                if m < 2:
                    for a in range(2):
                        block = 2 * p + a
                        row = 8 * a + 2 * m + 1
                        edge[block + 2, m : m + 1, cols] = tail[row : row + 1]
                        edge[block, 2 + m : 3 + m, cols] = found[base + 80 * a : base + 80 * a + 1]
        for p in range(4):
            back[p, 704:720, cols] = tails[p].astype(BF16)

    def inverse(rows):
        zero = dot(rows[:, 0:256], back_zero[...])
        two = dot(rows[:, 128:384], back_two[...])
        for n in range(2):
            even = zero + two if n == 0 else zero - two
            odd = dot(rows[:, 384:768], back_odd[:, 256 * n : 256 * n + 256])
            yield 2 * n, even + odd
            yield 2 * n + 4, even - odd

    for o, found in inverse(edge[1:9].reshape(64, 768).astype(BF16)):
        lanes = slice(128 * o, 128 * o + 256)
        halo[:, :, lanes] = found.reshape(8, 8, 256) + edge_in[1:9, :, lanes]

    @pl.loop(0, 4, unroll=4)
    def _(p):
        for first, found in inverse(back[p]):
            for half in range(2):
                o = first + half
                lanes = slice(128 * half, 128 * half + 128)
                for a in range(2):
                    d = 16 * p + 8 * a + o
                    for i in range(5):
                        for m in range(4):
                            at = 160 * m + 80 * a + 16 * i
                            to = 64 * i + 16 * m
                            out[d, to : to + 16, :] = (
                                found[at : at + 16, lanes] + got[d, to : to + 16, :].astype(F32)
                            ).astype(BF16)
                    for f in range(2):
                        at = 640 + 32 * f + 8 * a
                        to = 320 + 16 * f
                        pair = jnp.concatenate(
                            [found[at : at + 8, lanes], found[at + 16 : at + 24, lanes]], axis=0
                        )
                        out[d, to : to + 16, :] = (
                            pair + got[d, to : to + 16, :].astype(F32)
                        ).astype(BF16)
                    at = 704 + 8 * a
                    low = found[at : at + 8, lanes] + got[d, 352:360, :].astype(F32)
                    beyond = halo[2 * p + a, :, 128 * o : 128 * o + 128]
                    out[d, 352:368, :] = jnp.concatenate([low, beyond], axis=0).astype(BF16)


def spectral(got, lon, lat, weight):
    tables = list(lon) + [table.T for table in lon] + [lat.transpose(0, 2, 1), lat]
    return pl.pallas_call(
        spectral_kernel,
        in_specs=[vmem()] * 10,
        out_specs=[vmem(), vmem()],
        out_shape=[
            pltpu.VMEM((OWNERS, BACK, COLS), BF16),
            jax.ShapeDtypeStruct((2, LDEG), F32),
        ],
        scratch_shapes=[
            pltpu.VMEM((4, 4, 192, 768), BF16),
            pltpu.VMEM((4, LDEG, 768), BF16),
            pltpu.VMEM((4, 720, 768), BF16),
            pltpu.VMEM((10, 8, NLON), F32),
            pltpu.VMEM((10, 8, 768), F32),
            pltpu.VMEM((8, 8, NLON), F32),
        ],
        compiler_params=pltpu.CompilerParams(vmem_limit_bytes=20 * MIB),
        name="spectral",
    )(near(got), *[near(jnp.asarray(np.ascontiguousarray(table))) for table in tables], weight)


def spread(sent_back, i, field, held):
    base = pl.multiple_of(64 * i, 64) + 32 * field
    for ch in range(CH):
        at = base + 16 * (ch % 2)
        held[pl.ds(ch, 16, stride=PITCH), :] = sent_back[ch // 2, pl.ds(at, 16), :].astype(F32)


def spread_last(sent_back, field, held):
    for d in range(OWNERS):
        near = sent_back[d, 320 + 16 * field : 336 + 16 * field, :].astype(F32)
        last = sent_back[d, 352:368, :].astype(F32)
        for c in range(2):
            held[pl.ds(2 * d + c, 8, stride=PITCH), :] = near[8 * c : 8 * c + 8]
            for t in range(2):
                row = 4 * field + 2 * c + t
                at = (8 + t) * PITCH + 2 * d + c
                held[at : at + 1, :] = last[row : row + 1]


def unpack_rows(sent_back, field, out, held, staged, sems, visit):
    def send(i, rows):
        span = pl.ds(16 * i, rows)
        return pltpu.make_async_copy(staged.at[span], out.at[span], sems.at[i])

    @pl.loop(0, 5, unroll=5)
    def _(i):
        spread(sent_back, i, field, held)
        for r in range(16):
            staged[16 * i + r] = held[r * PITCH : r * PITCH + CH, :].astype(BF16)
            visit(16 * i + r)
        send(i, 16).start()

    spread_last(sent_back, field, held)
    for r in range(10):
        staged[80 + r] = held[r * PITCH : r * PITCH + CH, :].astype(BF16)
        visit(80 + r)
    send(5, 10).start()

    def finish():
        for i in range(6):
            send(i, 16 if i < 5 else 10).wait()

    return finish


def outside_rows(got_one, got_two):
    one, two = got_one[0], got_two[0]
    return jnp.where(even("lat"), two, one), jnp.where(even("lat"), one, two)


def unpack_flux_kernel(
    sent_back,
    weight,
    ocean,
    got_one,
    got_two,
    head,
    out,
    flux,
    to_group,
    to_near,
    to_far,
    held,
    staged,
    outside,
    found,
    sems,
):
    def put(row, cells):
        sums = jnp.dot(weight[...], cells, preferred_element_type=F32)
        found[pl.ds(4 * row, 4), :] = sums[0:4]

    finish = unpack_rows(
        sent_back, 0, out, held, staged, sems, lambda row: put(row + 1, staged[row])
    )
    for d in range(OWNERS):
        beyond = sent_back[d, 352:368, :].astype(F32)
        for side in range(2):
            outside[side, 2 * d : 2 * d + 2, :] = beyond[8 + 2 * side : 10 + 2 * side]
    put(0, outside[0].astype(BF16))
    put(91, outside[1].astype(BF16))

    lane = lax.broadcasted_iota(jnp.int32, (76, COLS), 1)

    def gather(row, cells, kept):
        at = lane == row
        return (
            jnp.where(at, pltpu.roll(cells, lax.rem(row + 1, COLS), 1), kept[0]),
            jnp.where(at, pltpu.roll(cells, row, 1), kept[1]),
        )

    blank = jnp.zeros((76, COLS), BF16)
    top, bottom = outside_rows(got_one, got_two)
    edges = gather(jnp.int32(0), top, (blank, blank))
    edges = gather(jnp.int32(91), bottom, edges)
    edges = lax.fori_loop(
        0, ROWS, lambda row, kept: gather(row + 1, ocean[row], kept), edges, unroll=18
    )

    sums = found[...].astype(BF16)
    flux[...] = sums
    near_edge = jnp.where(even("lon"), edges[0], edges[1])
    far_edge = jnp.where(even("lon"), edges[1], edges[0])
    for message, rows in ((to_near, near_edge), (to_far, far_edge), (to_group, head[...])):
        message[0:368, :] = sums
        message[368:448, :] = jnp.concatenate(
            [rows.astype(F32), jnp.zeros((4, COLS), F32)], axis=0
        ).astype(BF16)
    finish()


def unpack_taps_kernel(
    sent_back,
    weights,
    weights_other,
    ocean,
    got_one,
    got_two,
    out,
    taps,
    conv,
    held,
    staged,
    sems,
):
    finish = unpack_rows(sent_back, 1, out, held, staged, sems, lambda row: None)

    for half, given in enumerate((weights, weights_other)):
        rows = slice(128 * half, 128 * half + 128)
        wide = jnp.concatenate([given[...].astype(F32), jnp.zeros((48, 128), F32)], axis=0)
        conv[rows, :] = wide.T.astype(BF16)

    def build(row, cells):
        wide = jnp.concatenate([cells, jnp.zeros((4, COLS), BF16)], axis=0)
        base = pl.multiple_of(240 * row, 16)
        taps[pl.ds(base, 80), :] = pltpu.roll(wide, 1, 1)
        taps[pl.ds(base + 80, 80), :] = wide
        taps[pl.ds(base + 160, 80), :] = pltpu.roll(wide, COLS - 1, 1)

    top, bottom = outside_rows(got_one, got_two)
    build(0, top)
    build(91, bottom)
    taps[92 * 240 :, :] = jnp.zeros((48, COLS), BF16)

    @pl.loop(0, ROWS, unroll=18)
    def _(row):
        build(row + 1, ocean[row])

    finish()


def unpack_scratch():
    return [pltpu.VMEM((16 * PITCH, COLS), F32), pltpu.VMEM((ROWS, CH, COLS), BF16)]


def unpack_flux(sent_back, weight, ocean, top, bottom, head):
    return pl.pallas_call(
        unpack_flux_kernel,
        in_specs=[vmem()] * 6,
        out_specs=[in_hbm(), vmem(), vmem(), vmem(), vmem()],
        out_shape=[
            jax.ShapeDtypeStruct((ROWS, CH, COLS), BF16),
            jax.ShapeDtypeStruct((368, COLS), BF16),
            jax.ShapeDtypeStruct((448, COLS), BF16),
            jax.ShapeDtypeStruct((448, COLS), BF16),
            jax.ShapeDtypeStruct((448, COLS), BF16),
        ],
        scratch_shapes=unpack_scratch()
        + [
            pltpu.VMEM((2, CH, COLS), F32),
            pltpu.VMEM((368, COLS), F32),
            pltpu.SemaphoreType.DMA((6,)),
        ],
        compiler_params=pltpu.CompilerParams(vmem_limit_bytes=12 * MIB),
        name="unpack_flux",
    )(near(sent_back), weight, near(ocean), top, bottom, head)


def unpack_taps(sent_back, weights, weights_other, ocean, top, bottom):
    return pl.pallas_call(
        unpack_taps_kernel,
        in_specs=[vmem()] * 6,
        out_specs=[in_hbm(), vmem(), vmem()],
        out_shape=[
            jax.ShapeDtypeStruct((ROWS, CH, COLS), BF16),
            pltpu.VMEM((92 * 240 + 48, COLS), BF16),
            pltpu.VMEM((256, 768), BF16),
        ],
        scratch_shapes=unpack_scratch() + [pltpu.SemaphoreType.DMA((6,))],
        compiler_params=pltpu.CompilerParams(vmem_limit_bytes=12 * MIB),
        cost_estimate=pl.CostEstimate(flops=0, bytes_accessed=12_000_000, transcendentals=0),
        name="unpack_taps",
    )(near(sent_back), weights, weights_other, near(ocean), top, bottom)


def ocean_kernel(
    own,
    other,
    near_one,
    near_other,
    far_one,
    far_other,
    unfinished,
    conv,
    ocean,
    mask,
    out,
    taps,
    head,
    fluxes,
    hidden,
    staged,
    sems,
):
    def whole(one, two):
        total = one[0:368, :].astype(F32) + two[0:368, :].astype(F32)
        return total.astype(BF16).astype(F32)

    column = lax.broadcasted_iota(jnp.int32, (368, COLS), 1)
    def sides(one, two):
        return jnp.where(even("lon"), two, one), jnp.where(even("lon"), one, two)

    middle = whole(own, other)
    west, east = sides(whole(near_one, near_other), whole(far_one, far_other))
    west = pltpu.roll(west, 1, 1)
    east = pltpu.roll(east, COLS - 1, 1)
    fluxes[0] = jnp.where(column == 0, west, pltpu.roll(middle, 1, 1))
    fluxes[1] = middle
    fluxes[2] = jnp.where(column == COLS - 1, east, pltpu.roll(middle, COLS - 1, 1))

    head[:, 0:128] = own[368:448, :]
    head[:, 128:256] = other[368:448, :]

    lane = lax.broadcasted_iota(jnp.int32, (80, COLS), 1)
    first_edge, final_edge = sides(near_one[368:448, :], far_one[368:448, :])

    taps[92 * 240 :, :] = jnp.zeros((48, COLS), BF16)

    def complete(row):
        base = pl.multiple_of(240 * row, 16)
        first = pltpu.roll(first_edge, lax.rem(COLS - row, COLS), 1)
        final = pltpu.roll(final_edge, COLS - 1 - row, 1)
        shifts = (
            jnp.where(lane == 0, first, unfinished[pl.ds(base, 80), :]),
            unfinished[pl.ds(base + 80, 80), :],
            jnp.where(lane == COLS - 1, final, unfinished[pl.ds(base + 160, 80), :]),
        )
        for b, cells in enumerate(shifts):
            at = base + 80 * b
            taps[pl.ds(at, 64), :] = cells[0:64]
            rest = [cells[64:80].astype(F32)[0:12], fluxes[b, pl.ds(4 * row, 4), :]]
            taps[pl.ds(at + 64, 16), :] = jnp.concatenate(rest, axis=0).astype(BF16)

    def send(g):
        span = pl.ds(10 * g, 10)
        return pltpu.make_async_copy(staged.at[span], out.at[span], sems.at[g])

    def window(row):
        return taps[pl.ds(pl.multiple_of(240 * row, 16), 768), :]

    def convolve(g, more):
        for pair in range(5):
            first = 10 * g + 2 * pair
            around = jnp.concatenate([window(first), window(first + 1)], axis=1)
            x = jnp.dot(conv[...], around, preferred_element_type=F32)
            bent = jnp.tanh(x * (GELU_ONE + GELU_THREE * (x * x)))
            half = 0.5 * x
            hidden[lax.rem(g, 2), :, 256 * pair : 256 * pair + 256] = (half + half * bent).astype(
                BF16
            )
            if more:
                for k in range(2):
                    complete(first + 12 + k)

    def decode(g):
        delta = jnp.dot(head[...], hidden[lax.rem(g, 2)], preferred_element_type=F32)
        for k in range(10):
            row = 10 * g + k
            sea = mask[pl.ds(row, 1), :].astype(F32)
            staged[row] = (
                ocean[row].astype(F32) + sea * delta[0:76, COLS * k : COLS * k + COLS]
            ).astype(BF16)
        send(g).start()

    for row in range(12):
        complete(jnp.int32(row))
    convolve(jnp.int32(0), True)

    @pl.loop(1, 8, unroll=7)
    def _(g):
        convolve(g, True)
        decode(g - 1)

    convolve(jnp.int32(8), False)
    decode(jnp.int32(7))
    decode(jnp.int32(8))
    for g in range(9):
        send(g).wait()


def ocean_step(fluxes, taps, conv, ocean, sea_mask):
    return pl.pallas_call(
        ocean_kernel,
        in_specs=[vmem()] * 10,
        out_specs=in_hbm(),
        out_shape=jax.ShapeDtypeStruct((ROWS, 76, COLS), BF16),
        scratch_shapes=[
            pltpu.VMEM((92 * 240 + 48, COLS), BF16),
            pltpu.VMEM((80, 256), BF16),
            pltpu.VMEM((3, 368, COLS), F32),
            pltpu.VMEM((2, 256, 1280), BF16),
            pltpu.VMEM((ROWS, 76, COLS), BF16),
            pltpu.SemaphoreType.DMA((9,)),
        ],
        compiler_params=pltpu.CompilerParams(vmem_limit_bytes=14 * MIB),
        name="ocean",
    )(*fluxes, near(taps), near(conv), near(ocean), sea_mask)


def after(value, *others):
    return lax.optimization_barrier((value,) + others)[0]


def local(
    atmos,
    cotangent,
    ocean,
    sea_mask,
    spectral_weight,
    coupling,
    flux_weight,
    conv_weight,
    head_weight,
):
    atmos = atmos.transpose(1, 0, 2)
    cotangent = cotangent.transpose(1, 0, 2)
    ocean = ocean.transpose(1, 0, 2)
    near_pairs = [(k, k ^ 1) for k in range(8)]
    far_pairs = [(k, (k + 1 - 2 * (k % 2 == 0)) % 8) for k in range(8)]
    swap = [(0, 1), (1, 0)]
    lon_table, lat_table = make_tables(NLAT, NLON, KMODES, LDEG)

    barrier = lax.optimization_barrier
    sent, border_one, border_two = pack(atmos, cotangent, ocean, sea_mask, coupling)
    got = lax.all_to_all(sent, ("lat", "lon"), split_axis=0, concat_axis=0, tiled=True)

    conv = conv_weight.reshape(720, 128)
    got, conv, border_one, border_two = barrier((got, conv, border_one, border_two))
    conv_other = lax.ppermute(conv, "group", swap)
    got_one = lax.ppermute(border_one, "lat", near_pairs)
    got_two = lax.ppermute(border_two, "lat", [pair for pair in far_pairs if set(pair) != {0, 7}])
    sent_back, grad_spectral = spectral(
        got, arrange_lon(lon_table), arrange_lat(lat_table), spectral_weight
    )
    sent_back, conv_other, got_one, got_two = barrier(
        (sent_back, conv_other, got_one, got_two)
    )
    returned = lax.all_to_all(sent_back, ("lat", "lon"), split_axis=0, concat_axis=0, tiled=True)
    atmos_next, flux, to_group, to_near, to_far = unpack_flux(
        returned, flux_weight, ocean, got_one, got_two, head_weight.T
    )

    def crossed(pairs):
        return [(8 * g + k, 8 * (1 - g) + to) for g in range(2) for k, to in pairs]

    fluxes = [
        to_group,
        lax.ppermute(to_group, "group", swap),
        lax.ppermute(to_near, "lon", near_pairs),
        lax.ppermute(flux, ("group", "lon"), crossed(near_pairs)),
        lax.ppermute(to_far, "lon", far_pairs),
        lax.ppermute(flux, ("group", "lon"), crossed(far_pairs)),
    ]
    grad_atmos, taps, conv = unpack_taps(
        after(returned, flux), conv, conv_other, ocean, got_one, got_two
    )
    ocean_next = ocean_step(fluxes, taps, conv, ocean, sea_mask)
    return (
        atmos_next.transpose(1, 0, 2),
        grad_atmos.transpose(1, 0, 2),
        grad_spectral,
        ocean_next.transpose(1, 0, 2),
    )


def solution(mesh):
    in_specs = (
        P("group", "lat", "lon"),
        P("group", "lat", "lon"),
        P(None, "lat", "lon"),
        P("lat", "lon"),
        P(("group", "lat", "lon"), None),
        P("group"),
        P(None, "group"),
        P(None, None, None, "group"),
        P("group", None),
    )
    out_specs = (
        P("group", "lat", "lon"),
        P("group", "lat", "lon"),
        P(("group", "lat", "lon"), None),
        P(None, "lat", "lon"),
    )
    return jax.shard_map(local, mesh=mesh, in_specs=in_specs, out_specs=out_specs, check_vma=False)
```

```python
import math

import jax
import jax.numpy as jnp
import ml_dtypes
import numpy as np
from jax import lax
from jax.experimental import pallas as pl
from jax.experimental.pallas import tpu as pltpu
from jax.sharding import PartitionSpec as P

NLAT = 720
NLON = 1024
KMODES = 384
LDEG = 384
ROWS = 90
COLS = 128
CH = 128
OWNERS = 64
SENT = 360
BACK = 368
PITCH = CH + 1
F32 = jnp.float32
BF16 = jnp.bfloat16
MIB = 1024 * 1024
GELU_ONE = math.sqrt(2.0 / math.pi)
GELU_THREE = 0.044715 * GELU_ONE


def make_tables(nlat, nlon, kmodes, ldeg):
    column = np.arange(nlon, dtype=np.int64)[:, None]
    wavenum = np.arange(kmodes, dtype=np.int64)[None, :]
    step = np.float32(2.0 * math.pi / nlon)
    phase_cos = (column * wavenum % nlon).astype(np.float32) * step
    phase_sin = (column * (wavenum + 1) % nlon).astype(np.float32) * step
    lon_table = np.concatenate([np.cos(phase_cos), np.sin(phase_sin)], axis=1)
    lon_table = lon_table * np.float32(math.sqrt(2.0 / nlon))
    latrow = np.arange(nlat, dtype=np.int64)[:, None]
    degree = np.arange(ldeg, dtype=np.int64)[None, :]
    phase_lat = (degree * (2 * latrow + 1) % (4 * nlat)).astype(np.float32) * np.float32(
        math.pi / (2 * nlat)
    )
    lat_table = np.cos(phase_lat) * np.float32(math.sqrt(2.0 / nlat))
    return (lon_table.astype(ml_dtypes.bfloat16), lat_table.astype(ml_dtypes.bfloat16))


def arrange_lon(lon_table):
    cosines = np.arange(KMODES)
    sines = np.arange(1, KMODES + 1)
    place = np.concatenate([cosines, sines])
    zero = lon_table[:256, place % 4 == 0]
    two = lon_table[:256, place % 4 == 2]
    odd = lon_table[:512, place % 2 == 1]
    blank = np.zeros((256, 64), lon_table.dtype)
    return (
        np.concatenate([zero, blank], axis=1),
        np.concatenate([blank, two], axis=1),
        odd,
    )


def arrange_lat(lat_table):
    blocks = lat_table.reshape(4, 2, ROWS, LDEG)
    main = blocks[:, :, :80].reshape(4, 160, LDEG)
    middle = blocks[:, :, 80:88].reshape(4, 16, LDEG)
    last = blocks[:, :, 88:90]
    made = []
    for m in range(4):
        tail = np.zeros((4, 2, 4, 2, LDEG), lat_table.dtype)
        tail[:, :, m] = last
        tail = tail.reshape(4, 16, LDEG)
        made.append(np.concatenate([main, middle, tail], axis=1).reshape(768, LDEG))
    return np.stack(made)


def even(axis):
    return lax.rem(lax.axis_index(axis), 2) == 0


def pack_kernel(
    atmos,
    cotangent,
    ocean,
    mask,
    coupling,
    out,
    border_one,
    border_two,
    in_a,
    in_c,
    warm,
    sea_cells,
    gains,
    held_a,
    held_c,
    last,
    sems,
):
    def fetches(i, rows):
        span = pl.ds(16 * i, rows)
        return [
            pltpu.make_async_copy(atmos.at[span], in_a.at[span], sems.at[0, i]),
            pltpu.make_async_copy(cotangent.at[span], in_c.at[span], sems.at[1, i]),
        ]

    surface = [
        pltpu.make_async_copy(ocean.at[:, pl.ds(0, 16), :], warm, sems.at[2, 0]),
        pltpu.make_async_copy(mask, sea_cells, sems.at[2, 1]),
        pltpu.make_async_copy(coupling, gains, sems.at[2, 2]),
    ]
    facing = jnp.where(even("lat"), ROWS - 1, 0)
    others = [
        pltpu.make_async_copy(ocean.at[pl.ds(facing, 1)], border_one, sems.at[2, 5]),
        pltpu.make_async_copy(ocean.at[pl.ds(ROWS - 1 - facing, 1)], border_two, sems.at[3, 0]),
    ]
    for copy in surface:
        copy.start()
    for i in range(6):
        for copy in fetches(i, 16 if i < 5 else 10):
            copy.start()
    for copy in others:
        copy.start()
    for copy in surface:
        copy.wait()
    gain = jnp.broadcast_to(gains[...], (CH, COLS)).T

    def widen(i, rows):
        for copy in fetches(i, rows):
            copy.wait()
        for r in range(rows):
            row = 16 * i + r
            sea = sea_cells[pl.ds(row, 1), :].astype(F32)
            forcing = sea * warm[row].astype(F32)[0:1]
            held_a[r * PITCH : r * PITCH + CH, :] = in_a[row].astype(F32) + forcing * gain
            held_c[r * PITCH : r * PITCH + CH, :] = in_c[row].astype(F32)

    @pl.loop(0, 5)
    def _(i):
        widen(i, 16)
        base = pl.multiple_of(64 * i, 64)
        for ch in range(CH):
            for f, held in enumerate((held_a, held_c)):
                at = base + 32 * f + 16 * (ch % 2)
                out[ch // 2, pl.ds(at, 16), :] = held[pl.ds(ch, 16, stride=PITCH), :].astype(BF16)

    widen(5, 10)
    for d in range(OWNERS):
        for f, held in enumerate((held_a, held_c)):
            pair = [held[pl.ds(2 * d + c, 8, stride=PITCH), :] for c in range(2)]
            out[d, 320 + 16 * f : 336 + 16 * f, :] = jnp.concatenate(pair, axis=0).astype(BF16)
            for t in range(2):
                both = held[(8 + t) * PITCH + 2 * d : (8 + t) * PITCH + 2 * d + 2, :]
                for c in range(2):
                    row = 4 * f + 2 * c + t
                    last[d, row : row + 1, :] = both[c : c + 1]
        out[d, 352:360, :] = last[d].astype(BF16)

    for copy in others:
        copy.wait()


def vmem():
    return pl.BlockSpec(memory_space=pltpu.VMEM)


def near(array):
    return pltpu.with_memory_space_constraint(array, pltpu.VMEM)


def in_hbm():
    return pl.BlockSpec(memory_space=pltpu.HBM)


def pack(atmos, cotangent, ocean, sea_mask, coupling):
    given = (atmos, cotangent, ocean, sea_mask, coupling[None, :])
    return pl.pallas_call(
        pack_kernel,
        in_specs=[in_hbm()] * 5,
        out_specs=[vmem()] * 3,
        out_shape=[
            pltpu.VMEM((OWNERS, SENT, COLS), BF16),
            pltpu.VMEM((1, 76, COLS), BF16),
            pltpu.VMEM((1, 76, COLS), BF16),
        ],
        scratch_shapes=[
            pltpu.VMEM((ROWS, CH, COLS), BF16),
            pltpu.VMEM((ROWS, CH, COLS), BF16),
            pltpu.VMEM((ROWS, 16, COLS), BF16),
            pltpu.VMEM((ROWS, COLS), jnp.int32),
            pltpu.VMEM((1, CH), F32),
            pltpu.VMEM((16 * PITCH, COLS), F32),
            pltpu.VMEM((16 * PITCH, COLS), F32),
            pltpu.VMEM((OWNERS, 8, COLS), F32),
            pltpu.SemaphoreType.DMA((4, 6)),
        ],
        compiler_params=pltpu.CompilerParams(vmem_limit_bytes=14 * MIB),
        name="pack",
    )(*[pltpu.with_memory_space_constraint(array, pltpu.HBM) for array in given])


def spectral_kernel(
    got,
    lon_zero,
    lon_two,
    lon_odd,
    back_zero,
    back_two,
    back_odd,
    lat,
    lat_back,
    weight,
    out,
    grad,
    coef,
    kept,
    back,
    edge_in,
    edge,
    halo,
):
    edge_in[...] = jnp.zeros_like(edge_in)
    edge[...] = jnp.zeros_like(edge)

    def dot(one, two):
        return jnp.dot(one, two, preferred_element_type=F32)

    @pl.loop(0, 4, unroll=4)
    def _(p):
        found = []
        for a in range(2):
            first = 16 * p + 8 * a
            quarter = [
                jnp.concatenate([got[first + 2 * q + h].astype(F32) for h in range(2)], axis=1)
                for q in range(4)
            ]
            even_0 = quarter[0] + quarter[2]
            even_1 = quarter[1] + quarter[3]
            odd = jnp.concatenate(
                [(quarter[0] - quarter[2]).astype(BF16), (quarter[1] - quarter[3]).astype(BF16)],
                axis=1,
            )
            zero = dot((even_0 + even_1).astype(BF16), lon_zero[...])
            two = dot((even_0 - even_1).astype(BF16), lon_two[...])
            found.append(
                [
                    zero[:, 0:128],
                    zero[:, 128:256] + two[:, 0:128],
                    two[:, 128:256],
                    dot(odd, lon_odd[...]),
                ]
            )
        for n, cols in enumerate(
            (slice(0, 128), slice(128, 256), slice(256, 384), slice(384, 768))
        ):
            for m in range(4):
                for a in range(2):
                    for i in range(5):
                        coef[m, p, 80 * a + 16 * i : 80 * a + 16 * i + 16, cols] = found[a][n][
                            64 * i + 16 * m : 64 * i + 16 * m + 16
                        ].astype(BF16)
                coef[m, p, 160:176, cols] = jnp.concatenate(
                    [found[a][n][320 + 8 * m : 328 + 8 * m] for a in range(2)], axis=0
                ).astype(BF16)
                coef[m, p, 176:192, cols] = jnp.concatenate(
                    [found[a][n][352:360] for a in range(2)], axis=0
                ).astype(BF16)
        for a in range(2):
            block = 2 * p + a
            for o in range(8):
                lanes = slice(128 * o, 128 * o + 128)
                low = got[8 * block + o, 352:360, :].astype(F32)
                for c in range(2):
                    high = got[8 * block + o, 16 * c : 16 * c + 16, :].astype(F32)
                    edge_in[block + 2, c : c + 1, lanes] = low[2 * c + 1 : 2 * c + 2]
                    edge_in[block, 2 + c : 3 + c, lanes] = high[0:1]

    for c in range(2):
        scale = jnp.broadcast_to(weight[c : c + 1, :], (256, LDEG)).T
        total = jnp.zeros((LDEG, 128), F32)
        for n in range(3):
            cols = slice(256 * n, 256 * n + 256)
            spectra = []
            for f in range(2):
                m = 2 * f + c
                found = dot(lat[m], coef[m, :, :, cols].reshape(768, 256))
                kept[m, :, cols] = (found * scale).astype(BF16)
                spectra.append(found)
            product = spectra[0] * spectra[1]
            total = total + product[:, :128] + product[:, 128:]
        grad[c : c + 1, :] = jnp.sum(total.T, axis=0, keepdims=True) / KMODES
    for n in range(3):
        cols = slice(256 * n, 256 * n + 256)
        tails = [jnp.zeros((16, 256), F32) for _ in range(4)]
        for m in range(4):
            found = dot(lat_back[m], kept[m, :, cols])
            for p in range(4):
                base = 192 * p
                back[p, 160 * m : 160 * m + 160, cols] = found[base : base + 160].astype(BF16)
                back[p, 640 + 16 * m : 656 + 16 * m, cols] = found[
                    base + 160 : base + 176
                ].astype(BF16)
                tail = found[base + 176 : base + 192]
                tails[p] = tails[p] + tail
                if m < 2:
                    for a in range(2):
                        block = 2 * p + a
                        row = 8 * a + 2 * m + 1
                        edge[block + 2, m : m + 1, cols] = tail[row : row + 1]
                        edge[block, 2 + m : 3 + m, cols] = found[base + 80 * a : base + 80 * a + 1]
        for p in range(4):
            back[p, 704:720, cols] = tails[p].astype(BF16)

    def inverse(rows):
        zero = dot(rows[:, 0:256], back_zero[...])
        two = dot(rows[:, 128:384], back_two[...])
        for n in range(2):
            even = zero + two if n == 0 else zero - two
            odd = dot(rows[:, 384:768], back_odd[:, 256 * n : 256 * n + 256])
            yield 2 * n, even + odd
            yield 2 * n + 4, even - odd

    for o, found in inverse(edge[1:9].reshape(64, 768).astype(BF16)):
        lanes = slice(128 * o, 128 * o + 256)
        halo[:, :, lanes] = found.reshape(8, 8, 256) + edge_in[1:9, :, lanes]

    @pl.loop(0, 4, unroll=4)
    def _(p):
        for first, found in inverse(back[p]):
            for half in range(2):
                o = first + half
                lanes = slice(128 * half, 128 * half + 128)
                for a in range(2):
                    d = 16 * p + 8 * a + o
                    for i in range(5):
                        for m in range(4):
                            at = 160 * m + 80 * a + 16 * i
                            to = 64 * i + 16 * m
                            out[d, to : to + 16, :] = (
                                found[at : at + 16, lanes] + got[d, to : to + 16, :].astype(F32)
                            ).astype(BF16)
                    for f in range(2):
                        at = 640 + 32 * f + 8 * a
                        to = 320 + 16 * f
                        pair = jnp.concatenate(
                            [found[at : at + 8, lanes], found[at + 16 : at + 24, lanes]], axis=0
                        )
                        out[d, to : to + 16, :] = (
                            pair + got[d, to : to + 16, :].astype(F32)
                        ).astype(BF16)
                    at = 704 + 8 * a
                    low = found[at : at + 8, lanes] + got[d, 352:360, :].astype(F32)
                    beyond = halo[2 * p + a, :, 128 * o : 128 * o + 128]
                    out[d, 352:368, :] = jnp.concatenate([low, beyond], axis=0).astype(BF16)


def spectral(got, lon, lat, weight):
    tables = list(lon) + [table.T for table in lon] + [lat.transpose(0, 2, 1), lat]
    return pl.pallas_call(
        spectral_kernel,
        in_specs=[vmem()] * 10,
        out_specs=[vmem(), vmem()],
        out_shape=[
            pltpu.VMEM((OWNERS, BACK, COLS), BF16),
            jax.ShapeDtypeStruct((2, LDEG), F32),
        ],
        scratch_shapes=[
            pltpu.VMEM((4, 4, 192, 768), BF16),
            pltpu.VMEM((4, LDEG, 768), BF16),
            pltpu.VMEM((4, 720, 768), BF16),
            pltpu.VMEM((10, 8, NLON), F32),
            pltpu.VMEM((10, 8, 768), F32),
            pltpu.VMEM((8, 8, NLON), F32),
        ],
        compiler_params=pltpu.CompilerParams(vmem_limit_bytes=20 * MIB),
        name="spectral",
    )(near(got), *[near(jnp.asarray(np.ascontiguousarray(table))) for table in tables], weight)


def spread(sent_back, i, field, held):
    base = pl.multiple_of(64 * i, 64) + 32 * field
    for ch in range(CH):
        at = base + 16 * (ch % 2)
        held[pl.ds(ch, 16, stride=PITCH), :] = sent_back[ch // 2, pl.ds(at, 16), :].astype(F32)


def spread_last(sent_back, field, held):
    for d in range(OWNERS):
        near = sent_back[d, 320 + 16 * field : 336 + 16 * field, :].astype(F32)
        last = sent_back[d, 352:368, :].astype(F32)
        for c in range(2):
            held[pl.ds(2 * d + c, 8, stride=PITCH), :] = near[8 * c : 8 * c + 8]
            for t in range(2):
                row = 4 * field + 2 * c + t
                at = (8 + t) * PITCH + 2 * d + c
                held[at : at + 1, :] = last[row : row + 1]


def unpack_rows(sent_back, field, out, held, staged, sems, visit):
    def send(i, rows):
        span = pl.ds(16 * i, rows)
        return pltpu.make_async_copy(staged.at[span], out.at[span], sems.at[i])

    @pl.loop(0, 5, unroll=5)
    def _(i):
        spread(sent_back, i, field, held)
        for r in range(16):
            staged[16 * i + r] = held[r * PITCH : r * PITCH + CH, :].astype(BF16)
            visit(16 * i + r)
        send(i, 16).start()

    spread_last(sent_back, field, held)
    for r in range(10):
        staged[80 + r] = held[r * PITCH : r * PITCH + CH, :].astype(BF16)
        visit(80 + r)
    send(5, 10).start()

    def finish():
        for i in range(6):
            send(i, 16 if i < 5 else 10).wait()

    return finish


def outside_rows(got_one, got_two):
    one, two = got_one[0], got_two[0]
    return jnp.where(even("lat"), two, one), jnp.where(even("lat"), one, two)


def unpack_flux_kernel(
    sent_back,
    weight,
    ocean,
    got_one,
    got_two,
    head,
    out,
    flux,
    to_group,
    to_near,
    to_far,
    held,
    staged,
    outside,
    found,
    sems,
):
    def put(row, cells):
        sums = jnp.dot(weight[...], cells, preferred_element_type=F32)
        found[pl.ds(4 * row, 4), :] = sums[0:4]

    finish = unpack_rows(
        sent_back, 0, out, held, staged, sems, lambda row: put(row + 1, staged[row])
    )
    for d in range(OWNERS):
        beyond = sent_back[d, 352:368, :].astype(F32)
        for side in range(2):
            outside[side, 2 * d : 2 * d + 2, :] = beyond[8 + 2 * side : 10 + 2 * side]
    put(0, outside[0].astype(BF16))
    put(91, outside[1].astype(BF16))

    lane = lax.broadcasted_iota(jnp.int32, (76, COLS), 1)

    def gather(row, cells, kept):
        at = lane == row
        return (
            jnp.where(at, pltpu.roll(cells, lax.rem(row + 1, COLS), 1), kept[0]),
            jnp.where(at, pltpu.roll(cells, row, 1), kept[1]),
        )

    blank = jnp.zeros((76, COLS), BF16)
    top, bottom = outside_rows(got_one, got_two)
    edges = gather(jnp.int32(0), top, (blank, blank))
    edges = gather(jnp.int32(91), bottom, edges)
    edges = lax.fori_loop(
        0, ROWS, lambda row, kept: gather(row + 1, ocean[row], kept), edges, unroll=18
    )

    sums = found[0:368, :].astype(BF16)
    flux[...] = sums
    near_edge = jnp.where(even("lon"), edges[0], edges[1])
    far_edge = jnp.where(even("lon"), edges[1], edges[0])
    for message, rows in ((to_near, near_edge), (to_far, far_edge), (to_group, head[...])):
        message[0:368, :] = sums
        message[368:448, :] = jnp.concatenate(
            [rows.astype(F32), jnp.zeros((4, COLS), F32)], axis=0
        ).astype(BF16)
    finish()


def unpack_taps_kernel(
    sent_back,
    weights,
    weights_other,
    ocean,
    got_one,
    got_two,
    out,
    taps,
    conv,
    held,
    staged,
    sems,
):
    finish = unpack_rows(sent_back, 1, out, held, staged, sems, lambda row: None)

    for half, given in enumerate((weights, weights_other)):
        rows = slice(128 * half, 128 * half + 128)
        wide = jnp.concatenate([given[...].astype(F32), jnp.zeros((48, 128), F32)], axis=0)
        conv[rows, :] = wide.T.astype(BF16)

    def build(row, cells):
        wide = jnp.concatenate([cells, jnp.zeros((4, COLS), BF16)], axis=0)
        base = pl.multiple_of(240 * row, 16)
        taps[pl.ds(base, 80), :] = pltpu.roll(wide, 1, 1)
        taps[pl.ds(base + 80, 80), :] = wide
        taps[pl.ds(base + 160, 80), :] = pltpu.roll(wide, COLS - 1, 1)

    top, bottom = outside_rows(got_one, got_two)
    build(0, top)
    build(91, bottom)
    taps[92 * 240 :, :] = jnp.zeros((48, COLS), BF16)

    @pl.loop(0, ROWS, unroll=18)
    def _(row):
        build(row + 1, ocean[row])

    finish()


def unpack_scratch():
    return [pltpu.VMEM((16 * PITCH, COLS), F32), pltpu.VMEM((ROWS, CH, COLS), BF16)]


def unpack_flux(sent_back, weight, ocean, top, bottom, head):
    return pl.pallas_call(
        unpack_flux_kernel,
        in_specs=[vmem()] * 6,
        out_specs=[in_hbm(), vmem(), vmem(), vmem(), vmem()],
        out_shape=[
            jax.ShapeDtypeStruct((ROWS, CH, COLS), BF16),
            jax.ShapeDtypeStruct((368, COLS), BF16),
            jax.ShapeDtypeStruct((448, COLS), BF16),
            jax.ShapeDtypeStruct((448, COLS), BF16),
            jax.ShapeDtypeStruct((448, COLS), BF16),
        ],
        scratch_shapes=unpack_scratch()
        + [
            pltpu.VMEM((2, CH, COLS), F32),
            pltpu.VMEM((376, COLS), F32),
            pltpu.SemaphoreType.DMA((6,)),
        ],
        compiler_params=pltpu.CompilerParams(vmem_limit_bytes=12 * MIB),
        name="unpack_flux",
    )(near(sent_back), weight, near(ocean), top, bottom, head)


def unpack_taps(sent_back, weights, weights_other, ocean, top, bottom):
    return pl.pallas_call(
        unpack_taps_kernel,
        in_specs=[vmem()] * 6,
        out_specs=[in_hbm(), vmem(), vmem()],
        out_shape=[
            jax.ShapeDtypeStruct((ROWS, CH, COLS), BF16),
            pltpu.VMEM((92 * 240 + 48, COLS), BF16),
            pltpu.VMEM((256, 768), BF16),
        ],
        scratch_shapes=unpack_scratch() + [pltpu.SemaphoreType.DMA((6,))],
        compiler_params=pltpu.CompilerParams(vmem_limit_bytes=12 * MIB),
        cost_estimate=pl.CostEstimate(flops=0, bytes_accessed=12_000_000, transcendentals=0),
        name="unpack_taps",
    )(near(sent_back), weights, weights_other, near(ocean), top, bottom)


def ocean_kernel(
    own,
    other,
    near_one,
    near_other,
    far_one,
    far_other,
    unfinished,
    conv,
    ocean,
    mask,
    out,
    taps,
    head,
    fluxes,
    hidden,
    staged,
    sems,
):
    def whole(one, two):
        total = one[0:368, :].astype(F32) + two[0:368, :].astype(F32)
        return total.astype(BF16).astype(F32)

    column = lax.broadcasted_iota(jnp.int32, (368, COLS), 1)
    def sides(one, two):
        return jnp.where(even("lon"), two, one), jnp.where(even("lon"), one, two)

    middle = whole(own, other)
    west, east = sides(whole(near_one, near_other), whole(far_one, far_other))
    west = pltpu.roll(west, 1, 1)
    east = pltpu.roll(east, COLS - 1, 1)
    fluxes[0, 0:368, :] = jnp.where(column == 0, west, pltpu.roll(middle, 1, 1))
    fluxes[1, 0:368, :] = middle
    fluxes[2, 0:368, :] = jnp.where(column == COLS - 1, east, pltpu.roll(middle, COLS - 1, 1))

    head[:, 0:128] = own[368:448, :]
    head[:, 128:256] = other[368:448, :]

    lane = lax.broadcasted_iota(jnp.int32, (80, COLS), 1)
    first_edge, final_edge = sides(near_one[368:448, :], far_one[368:448, :])

    taps[92 * 240 :, :] = jnp.zeros((48, COLS), BF16)

    def complete(row):
        base = pl.multiple_of(240 * row, 16)
        first = pltpu.roll(first_edge, lax.rem(COLS - row, COLS), 1)
        final = pltpu.roll(final_edge, COLS - 1 - row, 1)
        shifts = (
            jnp.where(lane == 0, first, unfinished[pl.ds(base, 80), :]),
            unfinished[pl.ds(base + 80, 80), :],
            jnp.where(lane == COLS - 1, final, unfinished[pl.ds(base + 160, 80), :]),
        )
        for b, cells in enumerate(shifts):
            at = base + 80 * b
            taps[pl.ds(at, 64), :] = cells[0:64]
            rest = [cells[64:80].astype(F32)[0:12], fluxes[b, pl.ds(4 * row, 4), :]]
            taps[pl.ds(at + 64, 16), :] = jnp.concatenate(rest, axis=0).astype(BF16)

    def send(g):
        span = pl.ds(10 * g, 10)
        return pltpu.make_async_copy(staged.at[span], out.at[span], sems.at[g])

    def window(row):
        return taps[pl.ds(pl.multiple_of(240 * row, 16), 768), :]

    def convolve(g, more):
        for pair in range(5):
            first = 10 * g + 2 * pair
            around = jnp.concatenate([window(first), window(first + 1)], axis=1)
            x = jnp.dot(conv[...], around, preferred_element_type=F32)
            bent = jnp.tanh(x * (GELU_ONE + GELU_THREE * (x * x)))
            half = 0.5 * x
            hidden[lax.rem(g, 2), :, 256 * pair : 256 * pair + 256] = (half + half * bent).astype(
                BF16
            )
            if more:
                for k in range(2):
                    complete(first + 12 + k)

    def decode(g):
        delta = jnp.dot(head[...], hidden[lax.rem(g, 2)], preferred_element_type=F32)
        for k in range(10):
            row = 10 * g + k
            sea = mask[pl.ds(row, 1), :].astype(F32)
            staged[row] = (
                ocean[row].astype(F32) + sea * delta[0:76, COLS * k : COLS * k + COLS]
            ).astype(BF16)
        send(g).start()

    for row in range(12):
        complete(jnp.int32(row))
    convolve(jnp.int32(0), True)

    @pl.loop(1, 8, unroll=7)
    def _(g):
        convolve(g, True)
        decode(g - 1)

    convolve(jnp.int32(8), False)
    decode(jnp.int32(7))
    decode(jnp.int32(8))
    for g in range(9):
        send(g).wait()


def ocean_step(fluxes, taps, conv, ocean, sea_mask):
    return pl.pallas_call(
        ocean_kernel,
        in_specs=[vmem()] * 10,
        out_specs=in_hbm(),
        out_shape=jax.ShapeDtypeStruct((ROWS, 76, COLS), BF16),
        scratch_shapes=[
            pltpu.VMEM((92 * 240 + 48, COLS), BF16),
            pltpu.VMEM((80, 256), BF16),
            pltpu.VMEM((3, 376, COLS), F32),
            pltpu.VMEM((2, 256, 1280), BF16),
            pltpu.VMEM((ROWS, 76, COLS), BF16),
            pltpu.SemaphoreType.DMA((9,)),
        ],
        compiler_params=pltpu.CompilerParams(vmem_limit_bytes=14 * MIB),
        name="ocean",
    )(*fluxes, near(taps), near(conv), near(ocean), sea_mask)


def after(value, *others):
    return lax.optimization_barrier((value,) + others)[0]


def local(
    atmos,
    cotangent,
    ocean,
    sea_mask,
    spectral_weight,
    coupling,
    flux_weight,
    conv_weight,
    head_weight,
):
    atmos = atmos.transpose(1, 0, 2)
    cotangent = cotangent.transpose(1, 0, 2)
    ocean = ocean.transpose(1, 0, 2)
    near_pairs = [(k, k ^ 1) for k in range(8)]
    far_pairs = [(k, (k + 1 - 2 * (k % 2 == 0)) % 8) for k in range(8)]
    swap = [(0, 1), (1, 0)]
    lon_table, lat_table = make_tables(NLAT, NLON, KMODES, LDEG)

    barrier = lax.optimization_barrier
    sent, border_one, border_two = pack(atmos, cotangent, ocean, sea_mask, coupling)
    got = lax.all_to_all(sent, ("lat", "lon"), split_axis=0, concat_axis=0, tiled=True)

    conv = conv_weight.reshape(720, 128)
    got, conv, border_one, border_two = barrier((got, conv, border_one, border_two))
    conv_other = lax.ppermute(conv, "group", swap)
    got_one = lax.ppermute(border_one, "lat", near_pairs)
    got_two = lax.ppermute(border_two, "lat", [pair for pair in far_pairs if set(pair) != {0, 7}])
    sent_back, grad_spectral = spectral(
        got, arrange_lon(lon_table), arrange_lat(lat_table), spectral_weight
    )
    sent_back, conv_other, got_one, got_two = barrier(
        (sent_back, conv_other, got_one, got_two)
    )
    returned = lax.all_to_all(sent_back, ("lat", "lon"), split_axis=0, concat_axis=0, tiled=True)
    atmos_next, flux, to_group, to_near, to_far = unpack_flux(
        returned, flux_weight, ocean, got_one, got_two, head_weight.T
    )

    def crossed(pairs):
        return [(8 * g + k, 8 * (1 - g) + to) for g in range(2) for k, to in pairs]

    fluxes = [
        to_group,
        lax.ppermute(to_group, "group", swap),
        lax.ppermute(to_near, "lon", near_pairs),
        lax.ppermute(flux, ("group", "lon"), crossed(near_pairs)),
        lax.ppermute(to_far, "lon", far_pairs),
        lax.ppermute(flux, ("group", "lon"), crossed(far_pairs)),
    ]
    grad_atmos, taps, conv = unpack_taps(
        after(returned, flux), conv, conv_other, ocean, got_one, got_two
    )
    ocean_next = ocean_step(fluxes, taps, conv, ocean, sea_mask)
    return (
        atmos_next.transpose(1, 0, 2),
        grad_atmos.transpose(1, 0, 2),
        grad_spectral,
        ocean_next.transpose(1, 0, 2),
    )


def solution(mesh):
    in_specs = (
        P("group", "lat", "lon"),
        P("group", "lat", "lon"),
        P(None, "lat", "lon"),
        P("lat", "lon"),
        P(("group", "lat", "lon"), None),
        P("group"),
        P(None, "group"),
        P(None, None, None, "group"),
        P("group", None),
    )
    out_specs = (
        P("group", "lat", "lon"),
        P("group", "lat", "lon"),
        P(("group", "lat", "lon"), None),
        P(None, "lat", "lon"),
    )
    return jax.shard_map(local, mesh=mesh, in_specs=in_specs, out_specs=out_specs, check_vma=False)
```
